32 devices in a mesh: dp: 8 (over y, x, core), ctx: 4 (over z).
Axes of the slice: x: 2, y: 2, z: 4, core: 2. Of those that a mesh axis runs over, the one named last changes fastest.
Arguments:
- tokens: bfloat16 [64, 512, 1024], P('dp', 'ctx'), may hold values from -6 to 6
- lengths: int32 [64], P('dp'), may hold values from 128 to 512, as said below
- cotangent: bfloat16 [64, 512, 1024], P('dp', 'ctx'), may hold values from -6 to 6
- weight_query: bfloat16 [1024, 1024], P('dp', 'ctx'), may hold values from -0.1875 to 0.1875
- weight_key: bfloat16 [1024, 1024], P('dp', 'ctx'), may hold values from -0.1875 to 0.1875
- weight_value: bfloat16 [1024, 1024], P('dp', 'ctx'), may hold values from -0.1875 to 0.1875
- weight_out: bfloat16 [1024, 1024], P('dp', 'ctx'), may hold values from -0.75 to 0.75
- weight_inner: bfloat16 [1024, 4096], P('dp', 'ctx'), may hold values from -0.1875 to 0.1875
- weight_outer: bfloat16 [4096, 1024], P('dp', 'ctx'), may hold values from -0.09375 to 0.09375
- bias_query: float32 [1024], replicated, may hold values from -3 to 3
- bias_value: float32 [1024], replicated, may hold values from -3 to 3
- bias_out: float32 [1024], replicated, may hold values from -3 to 3
- bias_inner: float32 [4096], replicated, may hold values from -3 to 3
- bias_outer: float32 [1024], replicated, may hold values from -3 to 3
- gain_attn: float32 [1024], replicated, may hold values from 0.25 to 1.75
- shift_attn: float32 [1024], replicated, may hold values from -3 to 3
- gain_ffn: float32 [1024], replicated, may hold values from 0.25 to 1.75
- shift_ffn: float32 [1024], replicated, may hold values from -3 to 3
Outputs:
- mixed: bfloat16 [64, 512, 1024], P('dp', 'ctx')
- grad_tokens: float32 [64, 512, 1024], P('dp', 'ctx')
- grad_weight_query: float32 [1024, 1024], P('dp', 'ctx')
- grad_weight_key: float32 [1024, 1024], P('dp', 'ctx')
- grad_weight_value: float32 [1024, 1024], P('dp', 'ctx')
- grad_weight_out: float32 [1024, 1024], P('dp', 'ctx')
- grad_weight_inner: float32 [1024, 4096], P('dp', 'ctx')
- grad_weight_outer: float32 [4096, 1024], P('dp', 'ctx')
- grad_bias_query: float32 [1024], replicated
- grad_bias_value: float32 [1024], replicated
- grad_bias_out: float32 [1024], replicated
- grad_bias_inner: float32 [4096], replicated
- grad_bias_outer: float32 [1024], replicated
- grad_gain_attn: float32 [1024], replicated
- grad_shift_attn: float32 [1024], replicated
- grad_gain_ffn: float32 [1024], replicated
- grad_shift_ffn: float32 [1024], replicated
The draws below stay inside these ranges and needn't reach their ends.
Inputs may be any that keep to these rules, and one draw needn't show every extreme that they name: `lengths`: valid slots of each sequence; among the 8 sequences of each index of dp, one has all 512 slots valid.
All inputs are finite; a program needn't handle non-finite values.
Results may differ from the reference program's by a relative error of at most 0.012.
Values may be sent and summed in bfloat16 or wider, within the bound.
No kernel may reach another device: no remote copies, remote signals or barrier semaphores. Data moves between devices by JAX's collectives and lax.ppermute only.
A program may use at most 256 MiB of HBM per device.

```python
import math
import jax
import jax.numpy as jnp
from jax import lax

D = 1024
FF = 4096
HEADS = 16
HEAD_DIM = 64
SEQ_DEV = 8
SEQS = 64
SEQ_LEN = 512


def draw_lengths(key, part):
    key = jax.random.fold_in(key, 7)
    key_lengths, key_choice = jax.random.split(key)
    lengths_drawn = jax.random.randint(key_lengths, (SEQS,), SEQ_LEN // 4, SEQ_LEN + 1)
    group_count = SEQS // SEQ_DEV
    chosen_slot = jax.random.randint(key_choice, (group_count, 1), 0, SEQ_DEV)
    full_length = jnp.arange(SEQ_DEV)[None, :] == chosen_slot
    lengths_out = jnp.where(full_length, SEQ_LEN, lengths_drawn.reshape(group_count, SEQ_DEV))
    return lengths_out.reshape(SEQS).astype(jnp.int32)


def block_scale(key, extent, cuts, low, largest):
    def one(dim, parts):
        steps = jax.random.uniform(jax.random.fold_in(jax.random.fold_in(key, 6), dim), (parts,), jnp.float32, low / len(cuts), largest / len(cuts))
        return jnp.repeat(jnp.exp(steps), extent[dim] // parts).reshape((-1,) + (1,) * (len(extent) - dim - 1))

    loudness = one(*cuts[0])
    for cut in cuts[1:]:
        loudness = loudness * one(*cut)
    return loudness


def scatter_about(rng, extent, deviation, limit, shards=(), held_as=jnp.bfloat16):
    array = deviation * jax.random.normal(rng, extent, jnp.float32)
    if shards:
        array = array * block_scale(rng, extent, shards, -0.22, 0.18)
    return jnp.clip(array, -limit, limit).astype(held_as)


def setup_inputs(seed: int = 0) -> dict:
    arg_keys = jax.random.split(jax.random.key(seed), 19)
    return {
        "tokens": scatter_about(arg_keys[0], (SEQS, SEQ_LEN, D), 1.0, 6.0, ((0, 8), (1, 4))),
        "lengths": draw_lengths(jax.random.fold_in(arg_keys[18], 71), 0),
        "cotangent": scatter_about(arg_keys[2], (SEQS, SEQ_LEN, D), 1.0, 6.0, ((0, 8), (1, 4))),
        "weight_query": scatter_about(arg_keys[3], (D, D), D ** -0.5, 0.1875, ((0, 8), (1, 4))),
        "weight_key": scatter_about(arg_keys[4], (D, D), D ** -0.5, 0.1875, ((0, 8), (1, 4))),
        "weight_value": scatter_about(arg_keys[5], (D, D), D ** -0.5, 0.1875, ((0, 8), (1, 4))),
        "weight_out": scatter_about(arg_keys[6], (D, D), (D // 16) ** -0.5, 0.75, ((0, 8), (1, 4))),
        "weight_inner": scatter_about(arg_keys[7], (D, FF), D ** -0.5, 0.1875, ((0, 8), (1, 4))),
        "weight_outer": scatter_about(arg_keys[8], (FF, D), FF ** -0.5, 0.09375, ((0, 8), (1, 4))),
        "bias_query": scatter_about(arg_keys[9], (D,), 0.5, 3.0, (), jnp.float32),
        "bias_value": scatter_about(arg_keys[10], (D,), 0.5, 3.0, (), jnp.float32),
        "bias_out": scatter_about(arg_keys[11], (D,), 0.5, 3.0, (), jnp.float32),
        "bias_inner": scatter_about(arg_keys[12], (FF,), 0.5, 3.0, (), jnp.float32),
        "bias_outer": scatter_about(arg_keys[13], (D,), 0.5, 3.0, (), jnp.float32),
        "gain_attn": jnp.clip(1.0 + 0.15 * jax.random.normal(arg_keys[14], (D,), jnp.float32), 0.25, 1.75),
        "shift_attn": scatter_about(arg_keys[15], (D,), 0.5, 3.0, (), jnp.float32),
        "gain_ffn": jnp.clip(1.0 + 0.15 * jax.random.normal(arg_keys[16], (D,), jnp.float32), 0.25, 1.75),
        "shift_ffn": scatter_about(arg_keys[17], (D,), 0.5, 3.0, (), jnp.float32),
    }


@jax.custom_vjp
def low(v):
    return lax.optimization_barrier(v.astype(jnp.bfloat16)).astype(jnp.float32)

@jax.custom_vjp
def low_back(v):
    return v

def low_keep(v):
    return (low(v), None)

def low_pass(kept, grad):
    return (grad,)

def back_keep(v):
    return (v, None)

def back_low(kept, grad):
    return (low(grad),)
low.defvjp(low_keep, low_pass)
low_back.defvjp(back_keep, back_low)
epsilon = 1e-05
masked_score = -1000000000.0
score_scale = 0.125

def product(left_side, right_side):
    return jnp.dot(left_side, right_side, precision=lax.Precision.HIGHEST)

def layer_norm(summed, norm_gain, norm_shift):
    centred = summed - lax.optimization_barrier(jnp.mean(summed, axis=-1, keepdims=True))
    spread = lax.optimization_barrier(jnp.mean(centred * centred, axis=-1, keepdims=True))
    return centred * lax.rsqrt(spread + epsilon) * norm_gain + norm_shift

def forward(params, block, seq_lengths):
    w_query, w_key, w_value, w_out, w_inner, w_outer, b_query, b_value, b_out, b_inner, b_outer, gain_one, shift_one, gain_two, shift_two = params
    group_size, slot_count, width = block.shape
    query = low(low_back(product(block, w_query) + b_query)).reshape(group_size, slot_count, HEADS, HEAD_DIM)
    keys = low(low_back(product(block, w_key))).reshape(group_size, slot_count, HEADS, HEAD_DIM)
    values = low(low_back(product(block, w_value) + b_value)).reshape(group_size, slot_count, HEADS, HEAD_DIM)
    raw_scores = jnp.einsum('gqhd,gkhd->ghqk', query, keys, precision=lax.Precision.HIGHEST) * score_scale
    scores = low_back(raw_scores)
    key_valid = jnp.arange(slot_count)[None, :] < seq_lengths[:, None]
    scores = jnp.where(key_valid[:, None, None, :], scores, masked_score)
    top_score = lax.optimization_barrier(jnp.max(scores, axis=-1, keepdims=True))
    expo = jnp.exp(scores - top_score)
    probs = low(expo / lax.optimization_barrier(jnp.sum(expo, axis=-1, keepdims=True)))
    heads_out = jnp.einsum('ghqk,gkhd->gqhd', probs, values, precision=lax.Precision.HIGHEST)
    heads_out = low(low_back(heads_out.reshape(group_size, slot_count, width)))
    attended = low_back(product(heads_out, w_out) + b_out)
    hidden_one = layer_norm(block + attended, gain_one, shift_one)
    inner = low_back(product(low(hidden_one), w_inner) + b_inner)
    active = low(jax.nn.gelu(inner, approximate=False))
    outer = low_back(product(active, w_outer) + b_outer)
    return layer_norm(hidden_one + outer, gain_two, shift_two)

def reference(tokens, lengths, cotangent, weight_query, weight_key, weight_value, weight_out, weight_inner, weight_outer, bias_query, bias_value, bias_out, bias_inner, bias_outer, gain_attn, shift_attn, gain_ffn, shift_ffn):
    params = (weight_query.astype(jnp.float32), weight_key.astype(jnp.float32), weight_value.astype(jnp.float32), weight_out.astype(jnp.float32), weight_inner.astype(jnp.float32), weight_outer.astype(jnp.float32), bias_query.astype(jnp.float32), bias_value.astype(jnp.float32), bias_out.astype(jnp.float32), bias_inner.astype(jnp.float32), bias_outer.astype(jnp.float32), gain_attn.astype(jnp.float32), shift_attn.astype(jnp.float32), gain_ffn.astype(jnp.float32), shift_ffn.astype(jnp.float32))
    total_seqs, slot_count, width = tokens.shape
    group_size = math.gcd(total_seqs, max(1, 4096 // slot_count))
    block_count = total_seqs // group_size
    token_blocks = tokens.astype(jnp.float32).reshape(block_count, group_size, slot_count, width)
    cot_blocks = cotangent.astype(jnp.float32).reshape(block_count, group_size, slot_count, width)
    length_blocks = lengths.reshape(block_count, group_size).astype(jnp.int32)

    def one_group(carried, pieces):
        block, cot_block, lens_block = pieces
        valid = (jnp.arange(slot_count)[None, :] < lens_block[:, None]).astype(jnp.float32)

        def local_forward(param_tuple, token_block):
            return forward(param_tuple, token_block, lens_block)
        outputs, pull = jax.vjp(local_forward, params, block)
        grad_params, grad_block = pull(cot_block * valid[:, :, None])
        carried = jax.tree.map(jnp.add, carried, grad_params)
        return (carried, (outputs.astype(jnp.bfloat16), grad_block))
    zero_grads = jax.tree.map(jnp.zeros_like, params)
    grads, (mixed, grad_tokens) = lax.scan(one_group, zero_grads, (token_blocks, cot_blocks, length_blocks))
    mixed = mixed.reshape(total_seqs, slot_count, width)
    grad_tokens = grad_tokens.reshape(total_seqs, slot_count, width)
    return (mixed, grad_tokens, grads[0], grads[1], grads[2], grads[3], grads[4], grads[5], grads[6], grads[7], grads[8], grads[9], grads[10], grads[11], grads[12], grads[13], grads[14])
```

```python
import functools

import jax
import jax.numpy as jnp
from jax import lax
from jax.experimental import pallas as pl
from jax.experimental.pallas import tpu as pltpu
from jax.sharding import PartitionSpec as P

HEAD_DIM = 64
PAIR = 128
EPS = 1e-05
SCALE = 0.125
LOG2E = 1.4426950408889634
VMEM = 56 * 1024 * 1024

f32 = jnp.float32
bf16 = jnp.bfloat16


def params():
    return pltpu.CompilerParams(vmem_limit_bytes=VMEM)


def cost(flops, moved, special=0):
    return pl.CostEstimate(flops=int(flops), bytes_accessed=int(moved), transcendentals=int(special))


def mm(a, b):
    return jnp.dot(a, b, preferred_element_type=f32)


def mm_nt(a, b):
    return lax.dot_general(a, b, (((1,), (1,)), ((), ())), preferred_element_type=f32)


def mm_tn(a, b):
    return lax.dot_general(a, b, (((0,), (0,)), ((), ())), preferred_element_type=f32)


def place(parts, starts, out_shape, puts):
    count = len(puts)

    def kernel(starts_ref, *refs):
        ins, out, held, sems_in, sems_out = refs[: len(parts)], *refs[len(parts) :]
        arriving, leaving = [], []
        for n, (part, which, where) in enumerate(puts):
            arriving.append(pltpu.make_async_copy(ins[part], where(held, starts_ref[which]), sems_in.at[n]))
            arriving[-1].start()
        for n, (part, which, where) in enumerate(puts):
            start = starts_ref[which]
            arriving[n].wait()
            leaving.append(pltpu.make_async_copy(where(held, start), where(out, start), sems_out.at[n]))
            leaving[-1].start()
        for copy in leaving:
            copy.wait()

    size = sum(p.size * p.dtype.itemsize for p in parts)
    return pl.pallas_call(
        kernel,
        grid_spec=pltpu.PrefetchScalarGridSpec(
            num_scalar_prefetch=1,
            grid=(1,),
            in_specs=[pl.BlockSpec(memory_space=pl.ANY)] * len(parts),
            out_specs=pl.BlockSpec(memory_space=pl.ANY),
            scratch_shapes=[
                pltpu.VMEM(out_shape.shape, out_shape.dtype),
                pltpu.SemaphoreType.DMA((count,)),
                pltpu.SemaphoreType.DMA((count,)),
            ],
        ),
        out_shape=out_shape,
        compiler_params=params(),
        cost_estimate=cost(0, 2 * size),
    )(starts, *parts)


def attention_forward(qkv, lengths):
    seqs, slots, three = qkv.shape
    pairs = three // (3 * PAIR)

    def kernel(len_ref, qkv_ref, out_ref, lse_ref):
        valid_count = len_ref[pl.program_id(0)]
        q2 = qkv_ref[0, :, 0:PAIR]
        k2 = qkv_ref[0, :, PAIR : 2 * PAIR]
        vt = qkv_ref[0, :, 2 * PAIR : 3 * PAIR].T
        lane = lax.broadcasted_iota(jnp.int32, (slots, PAIR), 1)
        row = lax.broadcasted_iota(jnp.int32, (slots, slots), 0)
        halves = []
        for h in range(2):
            qh = jnp.where((lane < HEAD_DIM) == (h == 0), q2, jnp.zeros_like(q2))
            st = mm_nt(k2, qh) * (SCALE * LOG2E)
            st = jnp.where(row < valid_count, st, -1e30)
            top = jnp.max(st, axis=0, keepdims=True)
            p = jnp.exp2(st - top)
            total = jnp.sum(p, axis=0, keepdims=True)
            p_low = (p * (1.0 / total)).astype(bf16)
            halves.append(mm(vt[h * HEAD_DIM : (h + 1) * HEAD_DIM, :], p_low))
            lse_ref[0, 0, h : h + 1, :] = top + jnp.log2(total)
        out_ref[0] = jnp.concatenate(halves, axis=0).T.astype(bf16)

    grid_spec = pltpu.PrefetchScalarGridSpec(
        num_scalar_prefetch=1,
        grid=(seqs, pairs),
        in_specs=[pl.BlockSpec((1, slots, 3 * PAIR), lambda s, j, n: (s, 0, j))],
        out_specs=[
            pl.BlockSpec((1, slots, PAIR), lambda s, j, n: (s, 0, j)),
            pl.BlockSpec((1, 1, 2, slots), lambda s, j, n: (s, j, 0, 0)),
        ],
    )
    work = seqs * pairs * 2 * slots * slots
    return pl.pallas_call(
        kernel,
        grid_spec=grid_spec,
        out_shape=[
            jax.ShapeDtypeStruct((seqs, slots, pairs * PAIR), bf16),
            jax.ShapeDtypeStruct((seqs, pairs, 2, slots), f32),
        ],
        compiler_params=params(),
        cost_estimate=cost(work * 4 * PAIR * 2, qkv.size * 2.7, work),
    )(lengths, qkv)


def attention_backward(qkv, grad_heads, lse, lengths):
    seqs, slots, three = qkv.shape
    pairs = three // (3 * PAIR)

    def kernel(len_ref, qkv_ref, gh_ref, lse_ref, out_ref, sums_ref):
        valid_count = len_ref[pl.program_id(0)]
        q2 = qkv_ref[0, :, 0:PAIR]
        k2 = qkv_ref[0, :, PAIR : 2 * PAIR]
        v2 = qkv_ref[0, :, 2 * PAIR : 3 * PAIR]
        g2 = gh_ref[0]
        kt = k2.T
        lane = lax.broadcasted_iota(jnp.int32, (slots, PAIR), 1)
        row = lax.broadcasted_iota(jnp.int32, (slots, slots), 0)
        grad_k, grad_v, grad_q = [], [], []
        for h in range(2):
            mine = (lane < HEAD_DIM) == (h == 0)
            qh = jnp.where(mine, q2, jnp.zeros_like(q2))
            gh = jnp.where(mine, g2, jnp.zeros_like(g2))
            st = mm_nt(k2, qh) * (SCALE * LOG2E)
            p = jnp.exp2(st - lse_ref[0, 0, h : h + 1, :])
            p = jnp.where(row < valid_count, p, 0.0)
            dp = mm_nt(v2, gh)
            inner_sum = jnp.sum(p * dp, axis=0, keepdims=True)
            ds = (p * (dp - inner_sum)).astype(bf16)
            grad_v.append(mm(p.astype(bf16), g2))
            grad_k.append(mm(ds, q2))
            grad_q.append(mm(kt[h * HEAD_DIM : (h + 1) * HEAD_DIM, :], ds))
        gq = (jnp.concatenate(grad_q, axis=0).T * SCALE).astype(bf16)
        gk = (jnp.where(lane < HEAD_DIM, grad_k[0], grad_k[1]) * SCALE).astype(bf16)
        gv = jnp.where(lane < HEAD_DIM, grad_v[0], grad_v[1]).astype(bf16)
        out_ref[0, :, 0:PAIR] = gq
        out_ref[0, :, PAIR : 2 * PAIR] = gk
        out_ref[0, :, 2 * PAIR : 3 * PAIR] = gv
        sums_ref[0, 0, 0:1, :] = jnp.sum(gq.astype(f32), axis=0, keepdims=True)
        sums_ref[0, 0, 1:2, :] = jnp.sum(gv.astype(f32), axis=0, keepdims=True)

    grid_spec = pltpu.PrefetchScalarGridSpec(
        num_scalar_prefetch=1,
        grid=(seqs, pairs),
        in_specs=[
            pl.BlockSpec((1, slots, 3 * PAIR), lambda s, j, n: (s, 0, j)),
            pl.BlockSpec((1, slots, PAIR), lambda s, j, n: (s, 0, j)),
            pl.BlockSpec((1, 1, 2, slots), lambda s, j, n: (s, j, 0, 0)),
        ],
        out_specs=[
            pl.BlockSpec((1, slots, 3 * PAIR), lambda s, j, n: (s, 0, j)),
            pl.BlockSpec((1, 1, 2, PAIR), lambda s, j, n: (s, j, 0, 0)),
        ],
    )
    work = seqs * pairs * 2 * slots * slots
    return pl.pallas_call(
        kernel,
        grid_spec=grid_spec,
        out_shape=[
            jax.ShapeDtypeStruct((seqs, slots, three), bf16),
            jax.ShapeDtypeStruct((seqs, pairs, 2, PAIR), f32),
        ],
        compiler_params=params(),
        cost_estimate=cost(work * 10 * PAIR * 2, qkv.size * 5, work),
    )(lengths, qkv, grad_heads, lse)


def project(x, w, bias, cols=768):
    rows, depth = x.shape
    width = bias.shape[1]

    def kernel(x_ref, w_ref, b_ref, out_ref):
        out_ref[...] = (mm(x_ref[...], w_ref[...]) + b_ref[...]).astype(bf16)

    return pl.pallas_call(
        kernel,
        grid=(width // cols,),
        in_specs=[
            pl.BlockSpec((rows, depth), lambda j: (0, 0)),
            pl.BlockSpec((depth, cols), lambda j: (0, j)),
            pl.BlockSpec((1, cols), lambda j: (0, j)),
        ],
        out_specs=pl.BlockSpec((rows, cols), lambda j: (0, j)),
        out_shape=jax.ShapeDtypeStruct((rows, width), bf16),
        compiler_params=params(),
        cost_estimate=cost(2 * rows * depth * width, 2 * (x.size + depth * width + rows * width)),
    )(x, w, bias)


def normed(summed):
    centred = summed - jnp.mean(summed, axis=-1, keepdims=True)
    rstd = lax.rsqrt(jnp.mean(centred * centred, axis=-1, keepdims=True) + EPS)
    return centred * rstd, rstd


def norm_back(grad_hat, hat, rstd):
    return rstd * (
        grad_hat
        - jnp.mean(grad_hat, axis=-1, keepdims=True)
        - hat * jnp.mean(grad_hat * hat, axis=-1, keepdims=True)
    )


def out_forward(heads, w_attn, x, b_out, gain, shift, rows=256):
    total, width = x.shape

    def kernel(h_ref, w_ref, x_ref, b_ref, g_ref, s_ref, hat_ref, rstd_ref, low_ref):
        summed = mm(h_ref[...], w_ref[...]) + b_ref[...] + x_ref[...].astype(f32)
        hat, rstd = normed(summed)
        hat_ref[...] = hat
        rstd_ref[...] = rstd
        low_ref[...] = (hat * g_ref[...] + s_ref[...]).astype(bf16)

    block = pl.BlockSpec((rows, width), lambda i: (i, 0))
    vec = pl.BlockSpec((1, width), lambda i: (0, 0))
    return pl.pallas_call(
        kernel,
        grid=(total // rows,),
        in_specs=[block, pl.BlockSpec((width, width), lambda i: (0, 3)), block, vec, vec, vec],
        out_specs=[block, pl.BlockSpec((rows, 1), lambda i: (i, 0)), block],
        out_shape=[
            jax.ShapeDtypeStruct((total, width), f32),
            jax.ShapeDtypeStruct((total, 1), f32),
            jax.ShapeDtypeStruct((total, width), bf16),
        ],
        compiler_params=params(),
        cost_estimate=cost(2 * total * width * width, total * width * 10 + width * width * 2),
    )(heads, w_attn, x, b_out, gain, shift)


def gelu_pair(x):
    density = jnp.exp2(x * x * (-0.5 * LOG2E))
    t = 1.0 / (jnp.abs(x) * (0.3275911 * 0.7071067811865476) + 1.0)
    poly = 1.061405429 * 0.5
    for coefficient in (-1.453152027, 1.421413741, -0.284496736, 0.254829592):
        poly = poly * t + coefficient * 0.5
    tail = poly * t * density
    phi = jnp.where(x < 0, tail, 1.0 - tail)
    active = x * phi
    slope = phi + x * density * 0.3989422804014327
    return active, slope


def ffn_one(hidden, w_inner, b_inner, cols=512, chunk=256):
    rows, depth = hidden.shape
    width = w_inner.shape[1]

    def kernel(h_ref, w_ref, b_ref, act_ref, slope_ref):
        for c in range(rows // chunk):
            part = pl.ds(c * chunk, chunk)
            inner = mm(h_ref[part, :], w_ref[...]) + b_ref[...]
            active, slope = gelu_pair(inner)
            act_ref[part, :] = active.astype(bf16)
            slope_ref[part, :] = slope.astype(bf16)

    out = pl.BlockSpec((rows, cols), lambda j: (0, j))
    return pl.pallas_call(
        kernel,
        grid=(width // cols,),
        in_specs=[
            pl.BlockSpec((rows, depth), lambda j: (0, 0)),
            pl.BlockSpec((depth, cols), lambda j: (0, j)),
            pl.BlockSpec((1, cols), lambda j: (0, j)),
        ],
        out_specs=[out, out],
        out_shape=[jax.ShapeDtypeStruct((rows, width), bf16)] * 2,
        compiler_params=params(),
        cost_estimate=cost(2 * rows * depth * width, 2 * (hidden.size + w_inner.size + 2 * rows * width), 2 * rows * width),
    )(hidden, w_inner, b_inner)


def ffn_two(active, w_outer, hat_one, cot, lengths, vectors, slots, rows=256):
    total, depth = active.shape
    width = w_outer.shape[1]
    per_seq = slots // rows

    def kernel(len_ref, a_ref, w_ref, hat_ref, cot_ref, vec_ref, mixed_ref, grad_ref, low_ref, sums_ref):
        i = pl.program_id(0)
        g_one, s_one, b_outer, g_two, s_two = (vec_ref[k : k + 1, :] for k in range(5))
        summed = mm(a_ref[...], w_ref[...]) + b_outer + (hat_ref[...] * g_one + s_one)
        hat, rstd = normed(summed)
        mixed_ref[...] = (hat * g_two + s_two).astype(bf16)
        slot = (i % per_seq) * rows + lax.broadcasted_iota(jnp.int32, (rows, width), 0)
        grad_y = jnp.where(slot < len_ref[i // per_seq], cot_ref[...].astype(f32), 0.0)
        grad = norm_back(grad_y * g_two, hat, rstd)
        grad_ref[...] = grad
        low = grad.astype(bf16)
        low_ref[...] = low

        @pl.when(i == 0)
        def _():
            sums_ref[...] = jnp.zeros_like(sums_ref)

        sums_ref[0:1, :] += jnp.sum(grad_y * hat, axis=0, keepdims=True)
        sums_ref[1:2, :] += jnp.sum(grad_y, axis=0, keepdims=True)
        sums_ref[2:3, :] += jnp.sum(low.astype(f32), axis=0, keepdims=True)

    block = pl.BlockSpec((rows, width), lambda i, n: (i, 0))
    grid_spec = pltpu.PrefetchScalarGridSpec(
        num_scalar_prefetch=1,
        grid=(total // rows,),
        in_specs=[
            pl.BlockSpec((rows, depth), lambda i, n: (i, 0)),
            pl.BlockSpec(w_outer.shape, lambda i, n: (0, 0)),
            block,
            block,
            pl.BlockSpec((8, width), lambda i, n: (0, 0)),
        ],
        out_specs=[block, block, block, pl.BlockSpec((8, width), lambda i, n: (0, 0))],
    )
    return pl.pallas_call(
        kernel,
        grid_spec=grid_spec,
        out_shape=[
            jax.ShapeDtypeStruct((total, width), bf16),
            jax.ShapeDtypeStruct((total, width), f32),
            jax.ShapeDtypeStruct((total, width), bf16),
            jax.ShapeDtypeStruct((8, width), f32),
        ],
        compiler_params=params(),
        cost_estimate=cost(2 * total * width * depth, active.size * 2 + w_outer.size * 2 + total * width * 14),
    )(lengths, active, w_outer, hat_one, cot, vectors)


def ffn_back(grad_low, start, hidden_t, active, slope, w_outer, w_inner, order, cols=512):
    rows, width = grad_low.shape
    count = order.shape[0]
    half = width // 2

    def kernel(ord_ref, g_ref, start_ref, ht_ref, a_ref, s_ref, wo_ref, wi_ref, grad_ref, dwo_ref, dws_ref, dwk_ref, bias_ref):
        j = pl.program_id(0)
        grad = g_ref[...]
        grad_active = mm_nt(grad, wo_ref[...])
        inner = (grad_active * s_ref[...].astype(f32)).astype(bf16)
        bias_ref[...] = jnp.sum(inner.astype(f32), axis=0, keepdims=True)
        dwo_ref[...] = mm_tn(a_ref[...], grad).astype(bf16)
        dws_ref[...] = mm(ht_ref[0:half, :], inner).astype(bf16)
        dwk_ref[...] = mm(ht_ref[half:width, :], inner).astype(bf16)

        @pl.when(j == 0)
        def _():
            grad_ref[...] = start_ref[...]

        grad_ref[...] += mm_nt(inner, wi_ref[...])

    whole = lambda j, o: (0, 0)
    grid_spec = pltpu.PrefetchScalarGridSpec(
        num_scalar_prefetch=1,
        grid=(count,),
        in_specs=[
            pl.BlockSpec((rows, width), whole),
            pl.BlockSpec((rows, width), whole),
            pl.BlockSpec((width, rows), whole),
            pl.BlockSpec((rows, cols), lambda j, o: (0, o[j])),
            pl.BlockSpec((rows, cols), lambda j, o: (0, o[j])),
            pl.BlockSpec((cols, width), lambda j, o: (o[j], 0)),
            pl.BlockSpec((width, cols), lambda j, o: (0, o[j])),
        ],
        out_specs=[
            pl.BlockSpec((rows, width), whole),
            pl.BlockSpec((cols, width), lambda j, o: (j, 0)),
            pl.BlockSpec((half, cols), lambda j, o: (0, j)),
            pl.BlockSpec((half, cols), lambda j, o: (0, j)),
            pl.BlockSpec((1, cols), lambda j, o: (0, j)),
        ],
    )
    return pl.pallas_call(
        kernel,
        grid_spec=grid_spec,
        out_shape=[
            jax.ShapeDtypeStruct((rows, width), f32),
            jax.ShapeDtypeStruct((count * cols, width), bf16),
            jax.ShapeDtypeStruct((half, count * cols), bf16),
            jax.ShapeDtypeStruct((half, count * cols), bf16),
            jax.ShapeDtypeStruct((1, count * cols), f32),
        ],
        compiler_params=params(),
        cost_estimate=cost(8 * rows * width * count * cols, 12 * count * cols * width + 12 * rows * width),
    )(order, grad_low, start, hidden_t, active, slope, w_outer, w_inner)


def out_back(grad_hidden, hat, rstd, gain, w_attn, heads_s, heads_k, rows=256):
    total, width = grad_hidden.shape
    half = width // 2
    steps = total // rows

    def kernel(gh_ref, hat_ref, rstd_ref, gain_ref, w_ref, hs_ref, hk_ref, one_ref, heads_ref, dws_ref, dwk_ref, sums_ref, acc_s, acc_k):
        i = pl.program_id(0)
        grad_y = gh_ref[...]
        hat = hat_ref[...]
        grad = norm_back(grad_y * gain_ref[...], hat, rstd_ref[...])
        one_ref[...] = grad
        low = grad.astype(bf16)
        heads_ref[...] = mm_nt(low, w_ref[...]).astype(bf16)

        @pl.when(i == 0)
        def _():
            sums_ref[...] = jnp.zeros_like(sums_ref)
            acc_s[...] = jnp.zeros_like(acc_s)
            acc_k[...] = jnp.zeros_like(acc_k)

        acc_s[...] += mm_tn(hs_ref[...], low)
        acc_k[...] += mm_tn(hk_ref[...], low)
        sums_ref[0:1, :] += jnp.sum(grad_y * hat, axis=0, keepdims=True)
        sums_ref[1:2, :] += jnp.sum(grad_y, axis=0, keepdims=True)
        sums_ref[2:3, :] += jnp.sum(low.astype(f32), axis=0, keepdims=True)

        @pl.when(i == steps - 1)
        def _():
            dws_ref[...] = acc_s[...].astype(bf16)
            dwk_ref[...] = acc_k[...].astype(bf16)

    block = pl.BlockSpec((rows, width), lambda i: (i, 0))
    halfblock = pl.BlockSpec((rows, half), lambda i: (i, 0))
    whole = lambda i: (0, 0)
    return pl.pallas_call(
        kernel,
        grid=(steps,),
        in_specs=[
            block,
            block,
            pl.BlockSpec((rows, 1), lambda i: (i, 0)),
            pl.BlockSpec((1, width), whole),
            pl.BlockSpec((width, width), lambda i: (0, 3)),
            halfblock,
            halfblock,
        ],
        out_specs=[
            block,
            block,
            pl.BlockSpec((half, width), whole),
            pl.BlockSpec((half, width), whole),
            pl.BlockSpec((8, width), whole),
        ],
        out_shape=[
            jax.ShapeDtypeStruct((total, width), f32),
            jax.ShapeDtypeStruct((total, width), bf16),
            jax.ShapeDtypeStruct((half, width), bf16),
            jax.ShapeDtypeStruct((half, width), bf16),
            jax.ShapeDtypeStruct((8, width), f32),
        ],
        scratch_shapes=[pltpu.VMEM((half, width), f32), pltpu.VMEM((half, width), f32)],
        compiler_params=params(),
        cost_estimate=cost(4 * total * width * width, total * width * 16 + width * width * 4),
    )(grad_hidden, hat, rstd, gain, w_attn, heads_s, heads_k)


def token_grads(grad_qkv, w_attn, grad_one, rows=256):
    total, three = grad_qkv.shape
    width = grad_one.shape[1]

    def kernel(g_ref, w_ref, one_ref, out_ref):
        out_ref[...] = (mm_nt(g_ref[...], w_ref[...]) + one_ref[...]).astype(bf16)

    return pl.pallas_call(
        kernel,
        grid=(total // rows,),
        in_specs=[
            pl.BlockSpec((rows, three), lambda i: (i, 0)),
            pl.BlockSpec((width, three), lambda i: (0, 0)),
            pl.BlockSpec((rows, width), lambda i: (i, 0)),
        ],
        out_specs=pl.BlockSpec((rows, width), lambda i: (i, 0)),
        out_shape=jax.ShapeDtypeStruct((total, width), bf16),
        compiler_params=params(),
        cost_estimate=cost(2 * total * three * width, 2 * (total * three + width * three) + total * width * 6),
    )(grad_qkv, w_attn, grad_one)


def swap(array, axis, size, mask):
    return lax.ppermute(array, axis, [(i, i ^ mask) for i in range(size)])


def shift(array, axis, size, by):
    return lax.ppermute(array, axis, [(i, (i + by) % size) for i in range(size)])


def gather_columns(shard, c):
    near = swap(shard, "ctx", 4, 1)
    odd = (c & 1) == 1
    pair = jnp.stack([jnp.where(odd, near, shard), jnp.where(odd, shard, near)])
    across = lax.ppermute(pair, "ctx", [(1, 2), (2, 1)])
    outwards = lax.ppermute(across, "ctx", [(1, 0), (2, 3)])
    middle = (c == 1) | (c == 2)
    other = jnp.where(middle, across, outwards)
    upper = c >= 2
    return [
        jnp.where(upper, other[0], pair[0]),
        jnp.where(upper, other[1], pair[1]),
        jnp.where(upper, pair[0], other[0]),
        jnp.where(upper, pair[1], other[1]),
    ]


def gather_rows(block, r, dp):
    if dp != 8:
        return lax.all_gather(block, "dp", axis=0, tiled=True)
    rows, width = block.shape
    half = rows // 2
    by_x = swap(block, "dp", dp, 2)
    by_y = swap(block, "dp", dp, 4)
    far_top = swap(by_x[:half], "dp", dp, 4)
    far_low = swap(by_y[half:], "dp", dp, 2)
    own = [block, by_x, by_y, far_top, far_low]
    twin = [swap(part, "dp", dp, 1) for part in own]

    def at(offset, count):
        return lambda out, start: out.at[pl.ds(pl.multiple_of(start + offset, half), count), :]

    puts = []
    for n, base in ((0, 0), (5, 1)):
        puts += [
            (n, base, at(0, rows)),
            (n + 1, base ^ 2, at(0, rows)),
            (n + 2, base ^ 4, at(0, rows)),
            (n + 3, base ^ 6, at(0, half)),
            (n + 4, base ^ 6, at(half, half)),
        ]
    starts = jnp.stack([(r ^ m) * rows for m in range(8)]).astype(jnp.int32)
    return place(own + twin, starts, jax.ShapeDtypeStruct((dp * rows, width), block.dtype), puts)


def to_sequences(slots, c, ctx):
    seqs, count, width = slots.shape
    per = seqs // ctx
    parts = []
    for d in range(ctx):
        part = lax.dynamic_slice(slots, (((c + d) % ctx) * per, 0, 0), (per, count, width))
        parts.append(shift(part, "ctx", ctx, d) if d else part)
    starts = jnp.stack([((c - d) % ctx) * count for d in range(ctx)]).astype(jnp.int32)
    at = lambda out, start: out.at[:, pl.ds(pl.multiple_of(start, count), count), :]
    shape = jax.ShapeDtypeStruct((per, ctx * count, width), slots.dtype)
    return place(parts, starts, shape, [(d, d, at) for d in range(ctx)])


def to_slots(whole, c, ctx):
    per, total, width = whole.shape
    count = total // ctx
    parts = []
    for d in range(ctx):
        part = lax.dynamic_slice(whole, (0, ((c + d) % ctx) * count, 0), (per, count, width))
        parts.append(shift(part, "ctx", ctx, d) if d else part)
    starts = jnp.stack([((c - d) % ctx) * per for d in range(ctx)]).astype(jnp.int32)
    at = lambda out, start: out.at[pl.ds(start, per), :, :]
    shape = jax.ShapeDtypeStruct((per * ctx, count, width), whole.dtype)
    return place(parts, starts, shape, [(d, d, at) for d in range(ctx)])


def scatter_rows(parts, r, dp):
    y, x = (r >> 2) & 1, (r >> 1) & 1

    def pick(array, yi, xi, h):
        blocks, rows, width = array.shape
        array = array.reshape(2, 2, 2, rows // 2, width)
        start = (0 if yi is None else yi, 0 if xi is None else xi, h, 0, 0)
        sizes = (2 if yi is None else 1, 2 if xi is None else 1, 1, rows // 2, width)
        out = lax.dynamic_slice(array, tuple(jnp.int32(s) for s in start), sizes)
        return out.reshape(sizes[0] * sizes[1], rows // 2, width).astype(f32)

    def summed(yi, xi, h):
        return [pick(kept, yi, xi, h) + pick(got, yi, xi, h) for kept, got in parts]

    def pack(arrays):
        return jnp.concatenate([a.astype(bf16) for a in arrays], axis=-1)

    widths = [kept.shape[-1] for kept, _ in parts]

    def unpack(array):
        pieces, at = [], 0
        for width in widths:
            pieces.append(lax.slice_in_dim(array, at, at + width, axis=2).astype(f32))
            at += width
        return pieces

    def add(left, right):
        return [a + b for a, b in zip(left, right)]

    def one(array, index):
        return lax.dynamic_slice_in_dim(array, index, 1, axis=0)

    got_x = swap(pack(summed(None, 1 - x, 0)), "dp", dp, 2)
    got_y = swap(pack(summed(1 - y, None, 1)), "dp", dp, 4)
    top = swap(pack(add(summed(1 - y, x, 0), unpack(one(got_x, 1 - y)))), "dp", dp, 4)
    low = swap(pack(add(summed(y, 1 - x, 1), unpack(one(got_y, 1 - x)))), "dp", dp, 2)
    top = add(add(summed(y, x, 0), unpack(one(got_x, y))), unpack(top))
    low = add(add(summed(y, x, 1), unpack(one(got_y, x))), unpack(low))
    return [jnp.concatenate([a[0], b[0]], axis=0) for a, b in zip(top, low)]


def scatter_columns(blocks, c):
    sizes = [b.shape[1] // 4 for b in blocks]
    pair = c >> 1

    def pack(arrays):
        return jnp.concatenate([a.astype(bf16) for a in arrays], axis=1)

    def unpack(array, times):
        pieces, at = [], 0
        for size in sizes:
            pieces.append(array[:, at : at + times * size].astype(f32))
            at += times * size
        return pieces

    def columns(array, start, count):
        return lax.dynamic_slice_in_dim(array, start, count, axis=1)

    other = [columns(b, (1 - pair) * 2 * s, 2 * s) for b, s in zip(blocks, sizes)]
    got = lax.ppermute(pack(other), "ctx", [(0, 1), (3, 2)])
    other = [a + b for a, b in zip(other, unpack(got, 2))]
    got = lax.ppermute(pack(other), "ctx", [(1, 2), (2, 1)])
    mine = [columns(b, pair * 2 * s, 2 * s) + g for b, s, g in zip(blocks, sizes, unpack(got, 2))]
    odd = c & 1
    got = swap(pack([columns(m, (1 - odd) * s, s) for m, s in zip(mine, sizes)]), "ctx", 4, 1)
    return [columns(m, odd * s, s) + g for m, s, g in zip(mine, sizes, unpack(got, 1))]


def sum_everywhere(vector, dp, ctx):
    for axis, size in (("dp", dp), ("ctx", ctx)):
        mask = 1
        while mask < size:
            vector = vector + swap(vector, axis, size, mask)
            mask *= 2
    return vector


def pair_columns(query, key, value):
    rows, width = query.shape
    pieces = []
    for j in range(width // PAIR):
        pieces += [a[:, j * PAIR : (j + 1) * PAIR] for a in (query, key, value)]
    return jnp.concatenate(pieces, axis=1)


def on_device(
    dp,
    ctx,
    tokens,
    lengths,
    cotangent,
    weight_query,
    weight_key,
    weight_value,
    weight_out,
    weight_inner,
    weight_outer,
    bias_query,
    bias_value,
    bias_out,
    bias_inner,
    bias_outer,
    gain_attn,
    shift_attn,
    gain_ffn,
    shift_ffn,
):
    seq_total, slot_count, width = tokens.shape
    units = bias_inner.shape[0]
    per = seq_total // ctx
    slots = slot_count * ctx
    rows = per * slots
    c = lax.axis_index("ctx")
    r = lax.axis_index("dp")
    core = r & 1
    paired = dp == 8

    own_lengths = lax.dynamic_slice(lengths, (c * per,), (per,))
    attn_shard = jnp.concatenate([pair_columns(weight_query, weight_key, weight_value), weight_out], axis=1)
    split = attn_shard.shape[1] - weight_out.shape[1]

    pieces = gather_columns(attn_shard, c)
    block = jnp.concatenate([p[:, :split] for p in pieces] + [p[:, split:] for p in pieces], axis=1)
    x = to_sequences(tokens, c, ctx).reshape(rows, width)
    w_attn = gather_rows(block, r, dp)
    w_inner = gather_rows(jnp.concatenate(gather_columns(weight_inner, c), axis=1), r, dp)
    w_outer = gather_rows(jnp.concatenate(gather_columns(weight_outer, c), axis=1), r, dp)
    cot = to_sequences(cotangent, c, ctx).reshape(rows, width)

    bias_qkv = pair_columns(bias_query[None], jnp.zeros_like(bias_query)[None], bias_value[None])
    qkv = project(x, w_attn, bias_qkv).reshape(per, slots, 3 * width)
    heads, lse = attention_forward(qkv, own_lengths)
    heads = heads.reshape(rows, width)
    hat_one, rstd_one, hidden_low = out_forward(
        heads, w_attn, x, bias_out[None], gain_attn[None], shift_attn[None]
    )
    active, slope = ffn_one(hidden_low, w_inner, bias_inner[None])
    vectors = jnp.stack([gain_attn, shift_attn, bias_outer, gain_ffn, shift_ffn] + [shift_ffn] * 3)
    mixed, grad_two, grad_outer, sums_two = ffn_two(
        active, w_outer, hat_one, cot, own_lengths, vectors, slots
    )
    mixed = to_slots(mixed.reshape(per, slots, width), c, ctx)

    def split_features(array):
        count, features = array.shape
        if not paired:
            return array[:, : features // 2], array[:, features // 2 :]
        array = array.reshape(count, 4, 2, features // 8)
        halves = [
            lax.dynamic_slice_in_dim(array, which, 1, axis=2).reshape(count, features // 2)
            for which in (1 - core, core)
        ]
        return halves

    hidden_t = jnp.concatenate([h.T for h in split_features(hidden_low)], axis=0)
    if paired:
        order_s = (jnp.arange(4) * 2 + (1 - core)).astype(jnp.int32)
        order_k = (jnp.arange(4) * 2 + core).astype(jnp.int32)
    else:
        order_s, order_k = jnp.arange(4, dtype=jnp.int32), jnp.arange(4, 8, dtype=jnp.int32)
    grad_hidden, outer_s, inner_s1, inner_k1, bias_1 = ffn_back(
        grad_outer, grad_two, hidden_t, active, slope, w_outer, w_inner, order_s
    )
    grad_hidden, outer_k, inner_s2, inner_k2, bias_2 = ffn_back(
        grad_outer, grad_hidden, hidden_t, active, slope, w_outer, w_inner, order_k
    )
    heads_s, heads_k = split_features(heads)
    grad_one, grad_heads, out_s, out_k, sums_one = out_back(
        grad_hidden, hat_one, rstd_one, gain_attn[None], w_attn, heads_s, heads_k
    )
    grad_qkv, sums_qkv = attention_backward(qkv, grad_heads.reshape(per, slots, width), lse, own_lengths)
    grad_qkv = grad_qkv.reshape(rows, 3 * width)
    x_s, x_k = split_features(x)
    qkv_s = mm_tn(x_s, grad_qkv).astype(bf16)
    qkv_k = mm_tn(x_k, grad_qkv).astype(bf16)
    grad_tokens = token_grads(grad_qkv, w_attn, grad_one)
    grad_tokens = to_slots(grad_tokens.reshape(per, slots, width), c, ctx).astype(f32)

    if paired:

        def twin(sent, kept):
            blocks = kept.reshape(4, kept.shape[0] // 4, kept.shape[1])
            return (blocks, swap(sent, "dp", dp, 1).reshape(blocks.shape))

        (sum_outer,) = scatter_columns(scatter_rows([twin(outer_s, outer_k)], r, dp), c)
        inner_1, inner_2, sum_out = scatter_columns(
            scatter_rows([twin(inner_s2, inner_k1), twin(inner_s1, inner_k2), twin(out_s, out_k)], r, dp), c
        )
        sum_inner = jnp.where(
            core == 0,
            jnp.concatenate([inner_2, inner_1], axis=1),
            jnp.concatenate([inner_1, inner_2], axis=1),
        )
        (sum_qkv,) = scatter_columns(scatter_rows([twin(qkv_s, qkv_k)], r, dp), c)
        b_1, b_2 = bias_1.reshape(4, -1), bias_2.reshape(4, -1)
        bias_units = jnp.where(core == 0, jnp.stack([b_2, b_1], axis=1), jnp.stack([b_1, b_2], axis=1)).reshape(units)
    else:

        def over_dp(array):
            return lax.psum_scatter(array.astype(f32), "dp", scatter_dimension=0, tiled=True)

        inner_full = jnp.concatenate(
            [jnp.concatenate([inner_s1, inner_s2], axis=1), jnp.concatenate([inner_k1, inner_k2], axis=1)], axis=0
        )
        (sum_outer,) = scatter_columns([over_dp(jnp.concatenate([outer_s, outer_k], axis=0))], c)
        sum_inner, sum_out = scatter_columns(
            [over_dp(inner_full), over_dp(jnp.concatenate([out_s, out_k], axis=0))], c
        )
        (sum_qkv,) = scatter_columns([over_dp(jnp.concatenate([qkv_s, qkv_k], axis=0))], c)
        bias_units = jnp.concatenate([bias_1[0], bias_2[0]])

    own_rows = sum_qkv.shape[0]
    sum_qkv = sum_qkv.reshape(own_rows, -1, 3, PAIR)
    sum_query, sum_key, sum_value = (sum_qkv[:, :, k].reshape(own_rows, -1) for k in range(3))

    sums_qkv = jnp.sum(sums_qkv, axis=0)
    packed = jnp.concatenate(
        [
            sums_qkv[:, 0].reshape(-1),
            sums_qkv[:, 1].reshape(-1),
            sums_one[2],
            bias_units,
            sums_two[2],
            sums_one[0],
            sums_one[1],
            sums_two[0],
            sums_two[1],
        ]
    )
    packed = sum_everywhere(packed.reshape(-1, 128), dp, ctx).reshape(-1)
    totals, at = [], 0
    for size in (width, width, width, units, width, width, width, width, width):
        totals.append(packed[at : at + size])
        at += size
    return (mixed, grad_tokens, sum_query, sum_key, sum_value, sum_out, sum_inner, sum_outer, *totals)


def solution(mesh):
    rows = P("dp", "ctx", None)
    matrix = P("dp", "ctx")
    in_specs = (rows, P("dp"), rows) + (matrix,) * 6 + (P(),) * 9
    out_specs = (rows, rows) + (matrix,) * 6 + (P(),) * 9
    step = functools.partial(on_device, mesh.shape["dp"], mesh.shape["ctx"])
    return jax.shard_map(step, mesh=mesh, in_specs=in_specs, out_specs=out_specs, check_vma=False)
```

```python
import functools

import jax
import jax.numpy as jnp
from jax import lax
from jax.experimental import pallas as pl
from jax.experimental.pallas import tpu as pltpu
from jax.sharding import PartitionSpec as P

HEAD_DIM = 64
PAIR = 128
EPS = 1e-05
SCALE = 0.125
LOG2E = 1.4426950408889634
VMEM = 56 * 1024 * 1024

f32 = jnp.float32
bf16 = jnp.bfloat16


def params():
    return pltpu.CompilerParams(vmem_limit_bytes=VMEM)


def cost(flops, moved, special=0):
    return pl.CostEstimate(flops=int(flops * 12), bytes_accessed=int(moved * 12), transcendentals=int(special * 12))


ANY = pl.BlockSpec(memory_space=pl.ANY)


def mm(a, b):
    return jnp.dot(a, b, preferred_element_type=f32)


def mm_nt(a, b):
    return lax.dot_general(a, b, (((1,), (1,)), ((), ())), preferred_element_type=f32)


def mm_tn(a, b):
    return lax.dot_general(a, b, (((0,), (0,)), ((), ())), preferred_element_type=f32)


def place(parts, starts, out_shape, puts):
    count = len(puts)

    def kernel(starts_ref, *refs):
        ins, out, held, sems_in, sems_out = refs[: len(parts)], *refs[len(parts) :]
        arriving, leaving = [], []
        for n, (part, which, where) in enumerate(puts):
            arriving.append(pltpu.make_async_copy(ins[part], where(held, starts_ref[which]), sems_in.at[n]))
            arriving[-1].start()
        for n, (part, which, where) in enumerate(puts):
            start = starts_ref[which]
            arriving[n].wait()
            leaving.append(pltpu.make_async_copy(where(held, start), where(out, start), sems_out.at[n]))
            leaving[-1].start()
        for copy in leaving:
            copy.wait()

    size = sum(p.size * p.dtype.itemsize for p in parts)
    return pl.pallas_call(
        kernel,
        grid_spec=pltpu.PrefetchScalarGridSpec(
            num_scalar_prefetch=1,
            grid=(1,),
            in_specs=[pl.BlockSpec(memory_space=pl.ANY)] * len(parts),
            out_specs=pl.BlockSpec(memory_space=pl.ANY),
            scratch_shapes=[
                pltpu.VMEM(out_shape.shape, out_shape.dtype),
                pltpu.SemaphoreType.DMA((count,)),
                pltpu.SemaphoreType.DMA((count,)),
            ],
        ),
        out_shape=out_shape,
        compiler_params=params(),
        cost_estimate=cost(0, 2 * size),
    )(starts, *parts)


def attention_forward(qkv, lengths):
    seqs, slots, three = qkv.shape
    pairs = three // (3 * PAIR)

    def kernel(len_ref, qkv_ref, out_ref, lse_ref):
        valid_count = len_ref[pl.program_id(0)]
        q2 = qkv_ref[0, :, 0:PAIR]
        k2 = qkv_ref[0, :, PAIR : 2 * PAIR]
        vt = qkv_ref[0, :, 2 * PAIR : 3 * PAIR].T
        lane = lax.broadcasted_iota(jnp.int32, (slots, PAIR), 1)
        row = lax.broadcasted_iota(jnp.int32, (slots, slots), 0)
        halves = []
        for h in range(2):
            qh = jnp.where((lane < HEAD_DIM) == (h == 0), q2, jnp.zeros_like(q2))
            st = mm_nt(k2, qh) * (SCALE * LOG2E)
            st = jnp.where(row < valid_count, st, -1e30)
            top = jnp.max(st, axis=0, keepdims=True)
            p = jnp.exp2(st - top)
            total = jnp.sum(p, axis=0, keepdims=True)
            p_low = (p * (1.0 / total)).astype(bf16)
            halves.append(mm(vt[h * HEAD_DIM : (h + 1) * HEAD_DIM, :], p_low))
            lse_ref[0, 0, h : h + 1, :] = top + jnp.log2(total)
        out_ref[0] = jnp.concatenate(halves, axis=0).T.astype(bf16)

    grid_spec = pltpu.PrefetchScalarGridSpec(
        num_scalar_prefetch=1,
        grid=(seqs, pairs),
        in_specs=[pl.BlockSpec((1, slots, 3 * PAIR), lambda s, j, n: (s, 0, j))],
        out_specs=[
            pl.BlockSpec((1, slots, PAIR), lambda s, j, n: (s, 0, j)),
            pl.BlockSpec((1, 1, 2, slots), lambda s, j, n: (s, j, 0, 0)),
        ],
    )
    work = seqs * pairs * 2 * slots * slots
    return pl.pallas_call(
        kernel,
        grid_spec=grid_spec,
        out_shape=[
            jax.ShapeDtypeStruct((seqs, slots, pairs * PAIR), bf16),
            jax.ShapeDtypeStruct((seqs, pairs, 2, slots), f32),
        ],
        compiler_params=params(),
        cost_estimate=cost(work * 4 * PAIR * 2, qkv.size * 2.7, work),
    )(lengths, qkv)


def attention_backward(qkv, grad_heads, lse, lengths, seq, waits=()):
    _, slots, three = qkv.shape
    pairs = three // (3 * PAIR)

    def kernel(len_ref, qkv_ref, gh_ref, lse_ref, *refs):
        out_ref, sums_ref = refs[-2:]
        valid_count = len_ref[seq]
        q2 = qkv_ref[0, :, 0:PAIR]
        k2 = qkv_ref[0, :, PAIR : 2 * PAIR]
        v2 = qkv_ref[0, :, 2 * PAIR : 3 * PAIR]
        g2 = gh_ref[...]
        kt = k2.T
        lane = lax.broadcasted_iota(jnp.int32, (slots, PAIR), 1)
        row = lax.broadcasted_iota(jnp.int32, (slots, slots), 0)
        grad_k, grad_v, grad_q = [], [], []
        for h in range(2):
            mine = (lane < HEAD_DIM) == (h == 0)
            qh = jnp.where(mine, q2, jnp.zeros_like(q2))
            gh = jnp.where(mine, g2, jnp.zeros_like(g2))
            st = mm_nt(k2, qh) * (SCALE * LOG2E)
            p = jnp.exp2(st - lse_ref[0, 0, h : h + 1, :])
            p = jnp.where(row < valid_count, p, 0.0)
            dp = mm_nt(v2, gh)
            inner_sum = jnp.sum(p * dp, axis=0, keepdims=True)
            ds = (p * (dp - inner_sum)).astype(bf16)
            grad_v.append(mm(p.astype(bf16), g2))
            grad_k.append(mm(ds, q2))
            grad_q.append(mm(kt[h * HEAD_DIM : (h + 1) * HEAD_DIM, :], ds))
        gq = (jnp.concatenate(grad_q, axis=0).T * SCALE).astype(bf16)
        gk = (jnp.where(lane < HEAD_DIM, grad_k[0], grad_k[1]) * SCALE).astype(bf16)
        gv = jnp.where(lane < HEAD_DIM, grad_v[0], grad_v[1]).astype(bf16)
        out_ref[:, 0:PAIR] = gq
        out_ref[:, PAIR : 2 * PAIR] = gk
        out_ref[:, 2 * PAIR : 3 * PAIR] = gv
        sums_ref[0, 0:1, :] = jnp.sum(gq.astype(f32), axis=0, keepdims=True)
        sums_ref[0, 1:2, :] = jnp.sum(gv.astype(f32), axis=0, keepdims=True)

    grid_spec = pltpu.PrefetchScalarGridSpec(
        num_scalar_prefetch=1,
        grid=(pairs,),
        in_specs=[
            pl.BlockSpec((1, slots, 3 * PAIR), lambda j, n: (seq, 0, j)),
            pl.BlockSpec((slots, PAIR), lambda j, n: (seq, j)),
            pl.BlockSpec((1, 1, 2, slots), lambda j, n: (seq, j, 0, 0)),
        ]
        + [ANY] * len(waits),
        out_specs=[
            pl.BlockSpec((slots, 3 * PAIR), lambda j, n: (0, j)),
            pl.BlockSpec((1, 2, PAIR), lambda j, n: (j, 0, 0)),
        ],
    )
    work = pairs * 2 * slots * slots
    return pl.pallas_call(
        kernel,
        grid_spec=grid_spec,
        out_shape=[
            jax.ShapeDtypeStruct((slots, three), bf16),
            jax.ShapeDtypeStruct((pairs, 2, PAIR), f32),
        ],
        compiler_params=params(),
        cost_estimate=cost(work * 10 * PAIR * 2, slots * three * 5, work),
    )(lengths, qkv, grad_heads, lse, *waits)


def project(x, w, bias, waits=(), cols=768):
    rows, depth = x.shape
    width = bias.shape[1]

    def kernel(x_ref, w_ref, b_ref, *refs):
        refs[-1][...] = (mm(x_ref[...], w_ref[...]) + b_ref[...]).astype(bf16)

    return pl.pallas_call(
        kernel,
        grid=(width // cols,),
        in_specs=[
            pl.BlockSpec((rows, depth), lambda j: (0, 0)),
            pl.BlockSpec((depth, cols), lambda j: (0, j)),
            pl.BlockSpec((1, cols), lambda j: (0, j)),
        ]
        + [ANY] * len(waits),
        out_specs=pl.BlockSpec((rows, cols), lambda j: (0, j)),
        out_shape=jax.ShapeDtypeStruct((rows, width), bf16),
        compiler_params=params(),
        cost_estimate=cost(2 * rows * depth * width, 2 * (x.size + depth * width + rows * width)),
    )(x, w, bias, *waits)


def normed(summed):
    centred = summed - jnp.mean(summed, axis=-1, keepdims=True)
    rstd = lax.rsqrt(jnp.mean(centred * centred, axis=-1, keepdims=True) + EPS)
    return centred * rstd, rstd


def norm_back(grad_hat, hat, rstd):
    return rstd * (
        grad_hat
        - jnp.mean(grad_hat, axis=-1, keepdims=True)
        - hat * jnp.mean(grad_hat * hat, axis=-1, keepdims=True)
    )


def joined(w_ref, c, cols=slice(None)):
    part = w_ref[:, c, :, cols]
    return part.reshape(part.shape[0] * part.shape[1], part.shape[2])


def reordered(ref, features, first=0, count=8, block=128):
    parts = []
    for k in range(first, first + count):
        start = pl.multiple_of(features[k] * block, block)
        parts.append(ref[:, pl.ds(start, block)].T)
    return jnp.concatenate(parts, axis=0)


def out_forward(heads, w_mid, x, b_out, gain, shift, features, rows=256):
    total, width = x.shape
    blocks, ctx, depth, _ = w_mid.shape
    cols = width // ctx

    def kernel(feat_ref, h_ref, w_ref, x_ref, b_ref, g_ref, s_ref, hat_ref, rstd_ref, low_ref, turned_ref):
        h = h_ref[...]
        attended = jnp.concatenate([mm(h, joined(w_ref, c)) for c in range(ctx)], axis=1)
        summed = attended + b_ref[...] + x_ref[...].astype(f32)
        hat, rstd = normed(summed)
        hat_ref[...] = hat
        rstd_ref[...] = rstd
        low_ref[...] = (hat * g_ref[...] + s_ref[...]).astype(bf16)
        turned_ref[...] = reordered(low_ref, feat_ref)

    block = pl.BlockSpec((rows, width), lambda i, f: (i, 0))
    vec = pl.BlockSpec((1, width), lambda i, f: (0, 0))
    weight = pl.BlockSpec((blocks, ctx, depth, cols), lambda i, f: (0, 0, 0, 4))
    grid_spec = pltpu.PrefetchScalarGridSpec(
        num_scalar_prefetch=1,
        grid=(total // rows,),
        in_specs=[block, weight, block, vec, vec, vec],
        out_specs=[
            block,
            pl.BlockSpec((rows, 1), lambda i, f: (i, 0)),
            block,
            pl.BlockSpec((width, rows), lambda i, f: (0, i)),
        ],
    )
    return pl.pallas_call(
        kernel,
        grid_spec=grid_spec,
        out_shape=[
            jax.ShapeDtypeStruct((total, width), f32),
            jax.ShapeDtypeStruct((total, 1), f32),
            jax.ShapeDtypeStruct((total, width), bf16),
            jax.ShapeDtypeStruct((width, total), bf16),
        ],
        compiler_params=params(),
        cost_estimate=cost(2 * total * width * width, total * width * 12 + width * width * 2),
    )(features, heads, w_mid, x, b_out, gain, shift)


def gelu_pair(x):
    density = jnp.exp2(x * x * (-0.5 * LOG2E))
    t = 1.0 / (jnp.abs(x) * (0.3275911 * 0.7071067811865476) + 1.0)
    poly = 1.061405429 * 0.5
    for coefficient in (-1.453152027, 1.421413741, -0.284496736, 0.254829592):
        poly = poly * t + coefficient * 0.5
    tail = poly * t * density
    phi = jnp.where(x < 0, tail, 1.0 - tail)
    active = x * phi
    slope = phi + x * density * 0.3989422804014327
    return active, slope


def ffn_one(hidden, w_mid, b_inner, cols=512, chunk=256):
    rows, depth = hidden.shape
    width = b_inner.shape[1]
    blocks, ctx, deep, _ = w_mid.shape
    per = width // ctx // cols

    def kernel(h_ref, w_ref, b_ref, act_ref, slope_ref):
        w = joined(w_ref, 0)
        for c in range(rows // chunk):
            part = pl.ds(c * chunk, chunk)
            inner = mm(h_ref[part, :], w) + b_ref[...]
            active, slope = gelu_pair(inner)
            act_ref[part, :] = active.astype(bf16)
            slope_ref[part, :] = slope.astype(bf16)

    out = pl.BlockSpec((rows, cols), lambda j: (0, j))
    return pl.pallas_call(
        kernel,
        grid=(width // cols,),
        in_specs=[
            pl.BlockSpec((rows, depth), lambda j: (0, 0)),
            pl.BlockSpec((blocks, 1, deep, cols), lambda j: (0, j // per, 0, j % per)),
            pl.BlockSpec((1, cols), lambda j: (0, j)),
        ],
        out_specs=[out, out],
        out_shape=[jax.ShapeDtypeStruct((rows, width), bf16)] * 2,
        compiler_params=params(),
        cost_estimate=cost(2 * rows * depth * width, 2 * (hidden.size + depth * width + 2 * rows * width), 2 * rows * width),
    )(hidden, w_mid, b_inner)


def ffn_two(active, w_outer, hat_one, cot, lengths, vectors, slots, rows=256):
    total, depth = active.shape
    width = hat_one.shape[1]
    ctx = w_outer.shape[1]
    per_seq = slots // rows

    def kernel(len_ref, a_ref, w_ref, hat_ref, cot_ref, vec_ref, mixed_ref, grad_ref, low_ref, sums_ref):
        i = pl.program_id(0)
        g_one, s_one, b_outer, g_two, s_two = (vec_ref[k : k + 1, :] for k in range(5))
        a = a_ref[...]
        outer = jnp.concatenate([mm(a, joined(w_ref, c)) for c in range(ctx)], axis=1)
        summed = outer + b_outer + (hat_ref[...] * g_one + s_one)
        hat, rstd = normed(summed)
        mixed_ref[...] = (hat * g_two + s_two).astype(bf16)
        slot = (i % per_seq) * rows + lax.broadcasted_iota(jnp.int32, (rows, width), 0)
        grad_y = jnp.where(slot < len_ref[i // per_seq], cot_ref[...].astype(f32), 0.0)
        grad = norm_back(grad_y * g_two, hat, rstd)
        grad_ref[...] = grad
        low = grad.astype(bf16)
        low_ref[...] = low

        @pl.when(i == 0)
        def _():
            sums_ref[...] = jnp.zeros_like(sums_ref)

        sums_ref[0:1, :] += jnp.sum(grad_y * hat, axis=0, keepdims=True)
        sums_ref[1:2, :] += jnp.sum(grad_y, axis=0, keepdims=True)
        sums_ref[2:3, :] += jnp.sum(low.astype(f32), axis=0, keepdims=True)

    block = pl.BlockSpec((rows, width), lambda i, n: (i, 0))
    grid_spec = pltpu.PrefetchScalarGridSpec(
        num_scalar_prefetch=1,
        grid=(total // rows,),
        in_specs=[
            pl.BlockSpec((rows, depth), lambda i, n: (i, 0)),
            pl.BlockSpec(w_outer.shape, lambda i, n: (0, 0, 0, 0)),
            block,
            block,
            pl.BlockSpec((8, width), lambda i, n: (0, 0)),
        ],
        out_specs=[block, block, block, pl.BlockSpec((8, width), lambda i, n: (0, 0))],
    )
    return pl.pallas_call(
        kernel,
        grid_spec=grid_spec,
        out_shape=[
            jax.ShapeDtypeStruct((total, width), bf16),
            jax.ShapeDtypeStruct((total, width), f32),
            jax.ShapeDtypeStruct((total, width), bf16),
            jax.ShapeDtypeStruct((8, width), f32),
        ],
        compiler_params=params(),
        cost_estimate=cost(2 * total * width * depth, active.size * 2 + w_outer.size * 2 + total * width * 14),
    )(lengths, active, w_outer, hat_one, cot, vectors)


def ffn_back(grad_low, start, hidden_t, active, slope, w_outer, w_mid, order, waits=(), cols=512):
    rows, width = grad_low.shape
    count = order.shape[0]
    half = width // 2
    blocks, ctx, deep, _ = w_mid.shape
    per = active.shape[1] // ctx // cols
    outer_rows = w_outer.shape[2]
    outer_cols = w_outer.shape[3]

    def kernel(ord_ref, g_ref, start_ref, ht_ref, a_ref, s_ref, wo_ref, wi_ref, *refs):
        grad_ref, dwo_ref, dws_ref, dwk_ref, bias_ref = refs[-5:]
        j = pl.program_id(0)
        grad = g_ref[...]
        grad_active = sum(
            mm_nt(grad[:, c * outer_cols : (c + 1) * outer_cols], joined(wo_ref, c)) for c in range(ctx)
        )
        inner = (grad_active * s_ref[...].astype(f32)).astype(bf16)
        bias_ref[...] = jnp.sum(inner.astype(f32), axis=0, keepdims=True)
        dwo_ref[...] = mm_tn(a_ref[...], grad).astype(bf16)
        dws_ref[...] = mm(ht_ref[0:half, :], inner).astype(bf16)
        dwk_ref[...] = mm(ht_ref[half:width, :], inner).astype(bf16)

        @pl.when(j == 0)
        def _():
            grad_ref[...] = start_ref[...]

        grad_ref[...] += mm_nt(inner, joined(wi_ref, 0))

    whole = lambda j, o: (0, 0)
    grid_spec = pltpu.PrefetchScalarGridSpec(
        num_scalar_prefetch=1,
        grid=(count,),
        in_specs=[
            pl.BlockSpec((rows, width), whole),
            pl.BlockSpec((rows, width), whole),
            pl.BlockSpec((width, rows), whole),
            pl.BlockSpec((rows, cols), lambda j, o: (0, o[j])),
            pl.BlockSpec((rows, cols), lambda j, o: (0, o[j])),
            pl.BlockSpec((cols // outer_rows, ctx, outer_rows, outer_cols), lambda j, o: (o[j], 0, 0, 0)),
            pl.BlockSpec((blocks, 1, deep, cols), lambda j, o: (0, o[j] // per, 0, o[j] % per)),
        ]
        + [ANY] * len(waits),
        out_specs=[
            pl.BlockSpec((rows, width), whole),
            pl.BlockSpec((cols, width), lambda j, o: (j, 0)),
            pl.BlockSpec((half, cols), lambda j, o: (0, j)),
            pl.BlockSpec((half, cols), lambda j, o: (0, j)),
            pl.BlockSpec((1, cols), lambda j, o: (0, j)),
        ],
    )
    return pl.pallas_call(
        kernel,
        grid_spec=grid_spec,
        out_shape=[
            jax.ShapeDtypeStruct((rows, width), f32),
            jax.ShapeDtypeStruct((count * cols, width), bf16),
            jax.ShapeDtypeStruct((half, count * cols), bf16),
            jax.ShapeDtypeStruct((half, count * cols), bf16),
            jax.ShapeDtypeStruct((1, count * cols), f32),
        ],
        compiler_params=params(),
        cost_estimate=cost(8 * rows * width * count * cols, 12 * count * cols * width + 12 * rows * width),
    )(order, grad_low, start, hidden_t, active, slope, w_outer, w_mid, *waits)


def out_back(grad_hidden, hat, rstd, gain, w_mid, heads, features, waits=(), rows=256):
    total, width = grad_hidden.shape
    half = width // 2
    steps = total // rows
    blocks, ctx, depth, _ = w_mid.shape
    cols = width // ctx

    def kernel(feat_ref, gh_ref, hat_ref, rstd_ref, gain_ref, w_ref, h_ref, *refs):
        one_ref, heads_ref, dws_ref, dwk_ref, sums_ref, acc = refs[-6:]
        i = pl.program_id(0)
        grad_y = gh_ref[...]
        hat = hat_ref[...]
        grad = norm_back(grad_y * gain_ref[...], hat, rstd_ref[...])
        one_ref[...] = grad
        low = grad.astype(bf16)
        heads_ref[...] = sum(mm_nt(low[:, c * cols : (c + 1) * cols], joined(w_ref, c)) for c in range(ctx)).astype(bf16)

        @pl.when(i == 0)
        def _():
            sums_ref[...] = jnp.zeros_like(sums_ref)
            acc[...] = jnp.zeros_like(acc)

        acc[...] += mm(reordered(h_ref, feat_ref), low)
        sums_ref[0:1, :] += jnp.sum(grad_y * hat, axis=0, keepdims=True)
        sums_ref[1:2, :] += jnp.sum(grad_y, axis=0, keepdims=True)
        sums_ref[2:3, :] += jnp.sum(low.astype(f32), axis=0, keepdims=True)

        @pl.when(i == steps - 1)
        def _():
            dws_ref[...] = acc[0:half, :].astype(bf16)
            dwk_ref[...] = acc[half:width, :].astype(bf16)

    block = pl.BlockSpec((rows, width), lambda i, f: (i, 0))
    whole = lambda i, f: (0, 0)
    grid_spec = pltpu.PrefetchScalarGridSpec(
        num_scalar_prefetch=1,
        grid=(steps,),
        in_specs=[
            block,
            block,
            pl.BlockSpec((rows, 1), lambda i, f: (i, 0)),
            pl.BlockSpec((1, width), whole),
            pl.BlockSpec((blocks, ctx, depth, cols), lambda i, f: (0, 0, 0, 4)),
            block,
        ]
        + [ANY] * len(waits),
        out_specs=[
            block,
            block,
            pl.BlockSpec((half, width), whole),
            pl.BlockSpec((half, width), whole),
            pl.BlockSpec((8, width), whole),
        ],
        scratch_shapes=[pltpu.VMEM((width, width), f32)],
    )
    return pl.pallas_call(
        kernel,
        grid_spec=grid_spec,
        out_shape=[
            jax.ShapeDtypeStruct((total, width), f32),
            jax.ShapeDtypeStruct((total, width), bf16),
            jax.ShapeDtypeStruct((half, width), bf16),
            jax.ShapeDtypeStruct((half, width), bf16),
            jax.ShapeDtypeStruct((8, width), f32),
        ],
        compiler_params=params(),
        cost_estimate=cost(4 * total * width * width, total * width * 16 + width * width * 4),
    )(features, grad_hidden, hat, rstd, gain, w_mid, heads, *waits)


def attn_weight_grads(x, grads, features, part, got=None, waits=(), cols=768):
    total, width = x.shape
    count = len(grads)
    slots, three = grads[0].shape
    half = width // 2
    blocks = half // 128

    def kernel(feat_ref, x_ref, *refs):
        out_ref, turned = refs[-2:]

        @pl.when(pl.program_id(0) == 0)
        def _():
            turned[...] = reordered(x_ref, feat_ref, part * blocks, blocks)

        value = sum(mm(turned[:, n * slots : (n + 1) * slots], refs[n][...]) for n in range(count))
        if got is not None:
            value = value + refs[count][...].astype(f32)
        out_ref[...] = value.astype(bf16)

    column = pl.BlockSpec((slots, cols), lambda j, f: (0, j))
    out = pl.BlockSpec((half, cols), lambda j, f: (0, j))
    extra = [] if got is None else [got]
    grid_spec = pltpu.PrefetchScalarGridSpec(
        num_scalar_prefetch=1,
        grid=(three // cols,),
        in_specs=[pl.BlockSpec((total, width), lambda j, f: (0, 0))]
        + [column] * count
        + [out] * len(extra)
        + [ANY] * len(waits),
        out_specs=out,
        scratch_shapes=[pltpu.VMEM((half, total), bf16)],
    )
    return pl.pallas_call(
        kernel,
        grid_spec=grid_spec,
        out_shape=jax.ShapeDtypeStruct((half, three), bf16),
        compiler_params=params(),
        cost_estimate=cost(total * width * three, 2 * (total * width + total * three + width * three)),
    )(features, x, *grads, *extra, *waits)


def token_grads(grad_qkv, w_attn, grad_one, seq, waits=(), rows=256):
    slots, three = grad_qkv.shape
    width = grad_one.shape[1]
    steps = slots // rows

    def kernel(g_ref, w_ref, one_ref, *refs):
        refs[-1][...] = (mm_nt(g_ref[...], w_ref[...]) + one_ref[...]).astype(bf16)

    return pl.pallas_call(
        kernel,
        grid=(steps,),
        in_specs=[
            pl.BlockSpec((rows, three), lambda i: (i, 0)),
            pl.BlockSpec((width, three), lambda i: (0, 0)),
            pl.BlockSpec((rows, width), lambda i: (seq * steps + i, 0)),
        ]
        + [ANY] * len(waits),
        out_specs=pl.BlockSpec((rows, width), lambda i: (i, 0)),
        out_shape=jax.ShapeDtypeStruct((slots, width), bf16),
        compiler_params=params(),
        cost_estimate=cost(2 * slots * three * width, 2 * (slots * three + width * three) + slots * width * 6),
    )(grad_qkv, w_attn, grad_one, *waits)


def swap(array, axis, size, mask):
    return lax.ppermute(array, axis, [(i, i ^ mask) for i in range(size)])


def shift(array, axis, size, by):
    return lax.ppermute(array, axis, [(i, (i + by) % size) for i in range(size)])


def after(array, *earlier):
    return lax.optimization_barrier((array, *earlier))[0]


def after_all(array, earlier):
    return after(array, *earlier) if earlier else array


class Columns:
    def __init__(self, shard, c):
        self.c, self.shard = c, shard

    def first(self):
        self.near = swap(self.shard, "ctx", 4, 1)
        return self.near

    def second(self):
        odd = (self.c & 1) == 1
        self.pair = jnp.stack(
            [jnp.where(odd, self.near, self.shard), jnp.where(odd, self.shard, self.near)]
        )
        self.across = lax.ppermute(self.pair, "ctx", [(1, 2), (2, 1)])
        return self.across

    def third(self):
        self.outwards = lax.ppermute(self.across, "ctx", [(1, 0), (2, 3)])
        return self.outwards

    def pieces(self):
        middle = (self.c == 1) | (self.c == 2)
        other = jnp.where(middle, self.across, self.outwards)
        upper = self.c >= 2
        return jnp.concatenate([jnp.where(upper, other, self.pair), jnp.where(upper, self.pair, other)])


def gather_rows(block, r, dp):
    if dp != 8:
        return lax.all_gather(block, "dp", axis=0, tiled=True), ()
    rows, width = block.shape
    half = rows // 2
    by_x = swap(block, "dp", dp, 2)
    by_y = swap(block, "dp", dp, 4)
    far_top = swap(by_x[:half], "dp", dp, 4)
    far_low = swap(by_y[half:], "dp", dp, 2)
    own = [block, by_x, by_y, far_top, far_low]
    twin = [swap(part, "dp", dp, 1) for part in own]

    def at(offset, count):
        return lambda out, start: out.at[pl.ds(pl.multiple_of(start + offset, half), count), :]

    puts = []
    for n, base in ((0, 0), (5, 1)):
        puts += [
            (n, base, at(0, rows)),
            (n + 1, base ^ 2, at(0, rows)),
            (n + 2, base ^ 4, at(0, rows)),
            (n + 3, base ^ 6, at(0, half)),
            (n + 4, base ^ 6, at(half, half)),
        ]
    starts = jnp.stack([(r ^ m) * rows for m in range(8)]).astype(jnp.int32)
    shape = jax.ShapeDtypeStruct((dp * rows, width), block.dtype)
    return place(own + twin, starts, shape, puts), (by_x, by_y)


class Exchange:
    def __init__(self, array, c, ctx, gather):
        self.c, self.ctx, self.gather = c, ctx, gather
        if gather:
            seqs, self.count, self.width = array.shape
            self.per = seqs // ctx
        else:
            self.per, total, self.width = array.shape
            self.count = total // ctx
        self.dtype = array.dtype
        self.parts = [self.piece(array, (c + d) % ctx) for d in range(ctx)]
        self.pieces = tuple(self.parts)

    def piece(self, array, index):
        start = (index * self.per, 0, 0) if self.gather else (0, index * self.count, 0)
        return lax.dynamic_slice(array, start, (self.per, self.count, self.width))

    def send(self, *which):
        for d in which or range(1, self.ctx):
            self.parts[d] = shift(self.parts[d], "ctx", self.ctx, d)
        return self.parts

    def arrive(self, *earlier):
        self.parts = list(lax.optimization_barrier((*self.parts, *earlier))[: self.ctx])

    def placed(self):
        step = self.count if self.gather else self.per
        starts = jnp.stack([((self.c - d) % self.ctx) * step for d in range(self.ctx)]).astype(jnp.int32)
        if self.gather:
            at = lambda out, start: out.at[:, pl.ds(pl.multiple_of(start, step), step), :]
            shape = (self.per, self.ctx * self.count, self.width)
        else:
            at = lambda out, start: out.at[pl.ds(start, step), :, :]
            shape = (self.per * self.ctx, self.count, self.width)
        return place(self.parts, starts, jax.ShapeDtypeStruct(shape, self.dtype), [(d, d, at) for d in range(self.ctx)])


class RowSum:
    def __init__(self, parts, r, dp):
        self.parts, self.dp = parts, dp
        self.y, self.x = (r >> 2) & 1, (r >> 1) & 1
        self.widths = [kept.shape[-1] for _, kept in parts]

    def pick(self, array, yi, xi, h):
        _, rows, width = array.shape
        array = array.reshape(2, 2, 2, rows // 2, width)
        start = (0 if yi is None else yi, 0 if xi is None else xi, h, 0, 0)
        sizes = (2 if yi is None else 1, 2 if xi is None else 1, 1, rows // 2, width)
        out = lax.dynamic_slice(array, tuple(jnp.int32(s) for s in start), sizes)
        return out.reshape(sizes[0] * sizes[1], rows // 2, width).astype(f32)

    def summed(self, yi, xi, h):
        return [
            self.pick(kept, yi, xi, h) if got is None else self.pick(got, yi, xi, h) + self.pick(kept, yi, xi, h)
            for got, kept in self.parts
        ]

    def pack(self, arrays):
        return jnp.concatenate([a.astype(bf16) for a in arrays], axis=-1)

    def plus(self, arrays, packed, index=None):
        if index is not None:
            packed = lax.dynamic_slice_in_dim(packed, index, 1, axis=0)
        out, at = [], 0
        for array, width in zip(arrays, self.widths):
            out.append(array + lax.slice_in_dim(packed, at, at + width, axis=2).astype(f32))
            at += width
        return out

    def first_sends(self):
        self.sends = (self.pack(self.summed(None, 1 - self.x, 0)), self.pack(self.summed(1 - self.y, None, 1)))
        return self.sends

    def first(self):
        self.got_x = swap(self.sends[0], "dp", self.dp, 2)
        self.got_y = swap(self.sends[1], "dp", self.dp, 4)
        return (self.got_x, self.got_y)

    def first_there(self, *earlier):
        self.got_x, self.got_y = lax.optimization_barrier((self.got_x, self.got_y, *earlier))[:2]

    def second_there(self, *earlier):
        self.top, self.low = lax.optimization_barrier((self.top, self.low, *earlier))[:2]

    def second_sends(self):
        y, x = self.y, self.x
        self.sends = (
            self.pack(self.plus(self.summed(1 - y, x, 0), self.got_x, 1 - y)),
            self.pack(self.plus(self.summed(y, 1 - x, 1), self.got_y, 1 - x)),
        )
        return self.sends

    def second(self):
        self.top = swap(self.sends[0], "dp", self.dp, 4)
        self.low = swap(self.sends[1], "dp", self.dp, 2)
        return (self.top, self.low)

    def result(self):
        y, x = self.y, self.x
        top = self.plus(self.plus(self.summed(y, x, 0), self.got_x, y), self.top)
        low = self.plus(self.plus(self.summed(y, x, 1), self.got_y, x), self.low)
        return [jnp.concatenate([a[0], b[0]], axis=0) for a, b in zip(top, low)]


class ColumnSum:
    def __init__(self, blocks, c):
        self.blocks, self.c = blocks, c
        self.sizes = [b.shape[1] // 4 for b in blocks]
        self.pair, self.odd = c >> 1, c & 1

    def pack(self, arrays):
        return jnp.concatenate([a.astype(bf16) for a in arrays], axis=1)

    def unpack(self, array, times):
        pieces, at = [], 0
        for size in self.sizes:
            pieces.append(array[:, at : at + times * size].astype(f32))
            at += times * size
        return pieces

    def columns(self, arrays, index, times):
        return [
            lax.dynamic_slice_in_dim(a, index * times * s, times * s, axis=1) for a, s in zip(arrays, self.sizes)
        ]

    def first_send(self):
        self.other = self.columns(self.blocks, 1 - self.pair, 2)
        self.send = self.pack(self.other)
        return self.send

    def first(self):
        self.got = lax.ppermute(self.send, "ctx", [(0, 1), (3, 2)])
        return self.got

    def there(self, *earlier):
        self.got = after(self.got, *earlier)

    def second_send(self):
        self.send = self.pack([a + b for a, b in zip(self.other, self.unpack(self.got, 2))])
        return self.send

    def second(self):
        self.got = lax.ppermute(self.send, "ctx", [(1, 2), (2, 1)])
        return self.got

    def third_send(self):
        mine = self.columns(self.blocks, self.pair, 2)
        self.mine = [a + b for a, b in zip(mine, self.unpack(self.got, 2))]
        self.send = self.pack(self.columns(self.mine, 1 - self.odd, 1))
        return self.send

    def third(self):
        self.got = swap(self.send, "ctx", 4, 1)
        return self.got

    def result(self):
        return [a + b for a, b in zip(self.columns(self.mine, self.odd, 1), self.unpack(self.got, 1))]

    def whole(self):
        for stage in ("first", "second", "third"):
            getattr(self, stage + "_send")()
            getattr(self, stage)()
        return self.result()


def pair_columns(query, key, value):
    rows, width = query.shape
    pieces = []
    for j in range(width // PAIR):
        pieces += [a[:, j * PAIR : (j + 1) * PAIR] for a in (query, key, value)]
    return jnp.concatenate(pieces, axis=1)


def on_device(
    dp,
    ctx,
    tokens,
    lengths,
    cotangent,
    weight_query,
    weight_key,
    weight_value,
    weight_out,
    weight_inner,
    weight_outer,
    bias_query,
    bias_value,
    bias_out,
    bias_inner,
    bias_outer,
    gain_attn,
    shift_attn,
    gain_ffn,
    shift_ffn,
):
    seq_total, slot_count, width = tokens.shape
    units = bias_inner.shape[0]
    per = seq_total // ctx
    slots = slot_count * ctx
    rows = per * slots
    c = lax.axis_index("ctx")
    r = lax.axis_index("dp")
    core = r & 1
    paired = dp == 8

    own_lengths = lax.dynamic_slice(lengths, (c * per,), (per,))
    attn_shard = pair_columns(weight_query, weight_key, weight_value)
    attn = Columns(attn_shard, c)
    mid = Columns(jnp.concatenate([weight_inner, weight_out], axis=1), c)
    outer = Columns(weight_outer, c)
    attn.first()
    mid.shard = after(mid.shard, attn.near)
    attn.second()
    mid.first()
    attn.across, mid.near, outer.shard = lax.optimization_barrier((attn.across, mid.near, outer.shard))
    attn.third()
    mid.second()
    outer.first()
    attn.outwards, mid.across, outer.near, tokens = lax.optimization_barrier(
        (attn.outwards, mid.across, outer.near, tokens)
    )
    mid.third()
    outer.second()
    x = Exchange(tokens, c, ctx, True)
    x.send(2)
    block = jnp.concatenate([p for p in attn.pieces()], axis=1)
    w_attn, early = gather_rows(block, r, dp)
    x.parts[1], x.parts[3], mid.outwards, outer.across = lax.optimization_barrier(
        (x.parts[1], x.parts[3], mid.outwards, outer.across)
    )
    x.send(1, 3)
    w_mid = lax.all_gather(after_all(mid.pieces(), early), "dp", axis=0)
    outer.across = after(outer.across, x.parts[2])
    outer.third()
    x.arrive(outer.outwards)
    x = x.placed().reshape(rows, width)
    cot = Exchange(after(cotangent, x), c, ctx, True)
    cot.send()

    if paired:
        order_s = (jnp.arange(4) * 2 + (1 - core)).astype(jnp.int32)
        order_k = (jnp.arange(4) * 2 + core).astype(jnp.int32)
    else:
        order_s, order_k = jnp.arange(4, dtype=jnp.int32), jnp.arange(4, 8, dtype=jnp.int32)
    features = jnp.concatenate([order_s, order_k])

    bias_qkv = pair_columns(bias_query[None], jnp.zeros_like(bias_query)[None], bias_value[None])
    qkv = project(x, w_attn, bias_qkv, cot.pieces).reshape(per, slots, 3 * width)
    outer.outwards = after(outer.outwards, qkv)
    w_outer = lax.all_gather(outer.pieces(), "dp", axis=0)
    heads, lse = attention_forward(qkv, own_lengths)
    heads = heads.reshape(rows, width)
    hat_one, rstd_one, hidden_low, hidden_t = out_forward(
        heads, w_mid, x, bias_out[None], gain_attn[None], shift_attn[None], features
    )
    active, slope = ffn_one(hidden_low, w_mid, bias_inner[None])
    cot.arrive(hidden_low)
    cot = cot.placed().reshape(rows, width)
    vectors = jnp.stack([gain_attn, shift_attn, bias_outer, gain_ffn, shift_ffn] + [shift_ffn] * 3)
    mixed, grad_two, grad_outer, sums_two = ffn_two(
        active, w_outer, hat_one, cot, own_lengths, vectors, slots
    )
    mixed = Exchange(mixed.reshape(per, slots, width), c, ctx, False)
    mixed.send()

    def from_twin(sent):
        return swap(sent, "dp", dp, 1) if paired else sent

    def part(got, kept):
        blocks = (4, kept.shape[0] // 4, kept.shape[1])
        return (got.reshape(blocks), kept.reshape(blocks))

    grad_hidden, outer_s, inner_s1, inner_k1, bias_1 = ffn_back(
        grad_outer, grad_two, hidden_t, active, slope, w_outer, w_mid, order_s, mixed.pieces
    )
    got_outer = from_twin(outer_s)
    grad_hidden, outer_k, inner_s2, inner_k2, bias_2 = ffn_back(
        grad_outer, grad_hidden, hidden_t, active, slope, w_outer, w_mid, order_k, (mixed.parts[1],)
    )
    got_inner_1, got_inner_2 = from_twin(inner_s2), from_twin(inner_s1)
    hold = (mixed.parts[3],)
    if paired:
        sum_c = RowSum([part(after(got_outer, outer_k), outer_k)], r, dp)
        hold = (*hold, *sum_c.first_sends())
        sum_c.first()
    grad_one, grad_heads, out_s, out_k, sums_one = out_back(
        grad_hidden, hat_one, rstd_one, gain_attn[None], w_mid, heads, features, waits=hold
    )
    got_out = from_twin(out_s)
    got_inner_1, got_inner_2, out_k = lax.optimization_barrier((got_inner_1, got_inner_2, out_k))
    mixed.arrive(out_k)
    mixed = mixed.placed()
    grad_qkv, sums_qkv, slot_grads = [], [], []
    last = per - 1
    hold = (mixed, got_inner_1, got_inner_2)
    for n in range(per):
        grad, sums = attention_backward(qkv, grad_heads, lse, own_lengths, n, waits=hold)
        grad_qkv.append(grad)
        sums_qkv.append(sums)
        hold = ()
        if paired and n == 0:
            got_out = after(got_out, grad)
            sum_b = RowSum([part(got_inner_1, inner_k1), part(got_inner_2, inner_k2), part(got_out, out_k)], r, dp)
            sum_c.first_there(grad)
            hold = (*sum_c.second_sends(), *sum_b.first_sends())
            sum_c.second()
            sum_b.first()
        if n < last:
            tokens_n = token_grads(grad, w_attn, grad_one, n, waits=hold)
            slot_grads.append(Exchange(tokens_n[None], c, ctx, False))
            hold = slot_grads[-1].pieces
            if paired and n == 0:
                sum_c.second_there(tokens_n)
                hold = (*hold, sum_c.top, sum_c.low)
            slot_grads[-1].send()
    hold = []
    for exchange in slot_grads:
        exchange.arrive(grad_qkv[last])
        hold.append(exchange.placed())
    slot_grads = list(hold)
    if paired:
        cols_c = ColumnSum(sum_c.result(), c)
        sum_b.first_there(grad_qkv[last])
        hold = [*hold, after(cols_c.first_send(), grad_qkv[last]), *sum_b.second_sends()]
        cols_c.first()
        sum_b.second()
    qkv_s = attn_weight_grads(x, grad_qkv, features, 0, waits=hold)
    got_qkv = from_twin(qkv_s)
    hold = []
    if paired:
        cols_c.there(qkv_s)
        hold.append(cols_c.second_send())
        cols_c.second()
    tokens_n = token_grads(grad_qkv[last], w_attn, grad_one, last, waits=hold)
    slots_n = Exchange(tokens_n[None], c, ctx, False)
    slots_n.send()
    if paired:
        sum_b.second_there(tokens_n)
        cols_b = ColumnSum(sum_b.result(), c)
        cols_c.there(tokens_n)
        hold = (cols_b.first_send(), cols_c.third_send(), *slots_n.pieces)
        cols_b.first()
        cols_c.third()
        qkv_k = attn_weight_grads(x, grad_qkv, features, 1, after(got_qkv, tokens_n), hold)
        sum_a = RowSum([(None, qkv_k.reshape(4, qkv_k.shape[0] // 4, qkv_k.shape[1]))], r, dp)
        cols_c.there(qkv_k)
        sends = sum_a.first_sends()
        sum_a.first()
        cols_b.there(*sends)
        cols_b.second_send()
        cols_b.second()
        (sum_outer,) = cols_c.result()
        slots_n.arrive(cols_b.send)
        sum_a.first_there(cols_b.send, *slots_n.parts)
        sends = sum_a.second_sends()
        sum_a.second()
        cols_b.there(*sends)
        cols_b.third_send()
        cols_b.third()
        slots_n.arrive(cols_b.send)
        sum_a.second_there(cols_b.send)
        cols_a = ColumnSum(sum_a.result(), c)
        cols_a.first_send()
        cols_a.first()
    else:
        qkv_k = attn_weight_grads(x, grad_qkv, features, 1)
    slot_grads.append(slots_n.placed())
    grad_tokens = jnp.stack(slot_grads, axis=1)
    grad_tokens = grad_tokens.reshape(seq_total, slot_count, width).astype(f32)

    if paired:
        cols_b.there(cols_a.send)
        inner_1, inner_2, sum_out = cols_b.result()
        cols_a.second_send()
        cols_a.second()
        cols_a.third_send()
        cols_a.third()
        (sum_qkv,) = cols_a.result()
        sum_inner = jnp.where(
            core == 0,
            jnp.concatenate([inner_2, inner_1], axis=1),
            jnp.concatenate([inner_1, inner_2], axis=1),
        )
        b_1, b_2 = bias_1.reshape(4, -1), bias_2.reshape(4, -1)
        bias_units = jnp.where(core == 0, jnp.stack([b_2, b_1], axis=1), jnp.stack([b_1, b_2], axis=1)).reshape(units)
    else:

        def over_dp(*arrays):
            array = jnp.concatenate(arrays, axis=0)
            return lax.psum_scatter(array.astype(f32), "dp", scatter_dimension=0, tiled=True)

        inner_s, inner_k = jnp.concatenate([inner_s1, inner_s2], axis=1), jnp.concatenate([inner_k1, inner_k2], axis=1)
        (sum_outer,) = ColumnSum([over_dp(outer_s, outer_k)], c).whole()
        sum_inner, sum_out = ColumnSum([over_dp(inner_s, inner_k), over_dp(out_s, out_k)], c).whole()
        (sum_qkv,) = ColumnSum([over_dp(qkv_s, qkv_k)], c).whole()
        bias_units = jnp.concatenate([bias_1[0], bias_2[0]])

    own_rows = sum_qkv.shape[0]
    sum_qkv = sum_qkv.reshape(own_rows, -1, 3, PAIR)
    sum_query, sum_key, sum_value = (sum_qkv[:, :, k].reshape(own_rows, -1) for k in range(3))

    sums_qkv = sum(sums_qkv)
    packed = jnp.concatenate(
        [
            sums_qkv[:, 0].reshape(-1),
            sums_qkv[:, 1].reshape(-1),
            sums_one[2],
            bias_units,
            sums_two[2],
            sums_one[0],
            sums_one[1],
            sums_two[0],
            sums_two[1],
        ]
    )
    packed = lax.all_gather(packed.reshape(-1, 128), ("dp", "ctx"))
    if paired:
        packed = after(packed, cols_a.send)
    packed = jnp.sum(packed, axis=0).reshape(-1)
    totals, at = [], 0
    for size in (width, width, width, units, width, width, width, width, width):
        totals.append(packed[at : at + size])
        at += size
    return (mixed, grad_tokens, sum_query, sum_key, sum_value, sum_out, sum_inner, sum_outer, *totals)


def solution(mesh):
    rows = P("dp", "ctx", None)
    matrix = P("dp", "ctx")
    in_specs = (rows, P("dp"), rows) + (matrix,) * 6 + (P(),) * 9
    out_specs = (rows, rows) + (matrix,) * 6 + (P(),) * 9
    step = functools.partial(on_device, mesh.shape["dp"], mesh.shape["ctx"])
    return jax.shard_map(step, mesh=mesh, in_specs=in_specs, out_specs=out_specs, check_vma=False)
```

```python
import functools

import jax
import jax.numpy as jnp
from jax import lax
from jax.experimental import pallas as pl
from jax.experimental.pallas import tpu as pltpu
from jax.sharding import PartitionSpec as P

HEAD_DIM = 64
PAIR = 128
EPS = 1e-05
SCALE = 0.125
LOG2E = 1.4426950408889634
VMEM = 56 * 1024 * 1024

f32 = jnp.float32
bf16 = jnp.bfloat16


def params():
    return pltpu.CompilerParams(vmem_limit_bytes=VMEM)


def cost(flops, moved, special=0):
    return pl.CostEstimate(flops=int(flops * 12), bytes_accessed=int(moved * 12), transcendentals=int(special * 12))


ANY = pl.BlockSpec(memory_space=pl.ANY)


def mm(a, b):
    return jnp.dot(a, b, preferred_element_type=f32)


def mm_nt(a, b):
    return lax.dot_general(a, b, (((1,), (1,)), ((), ())), preferred_element_type=f32)


def mm_tn(a, b):
    return lax.dot_general(a, b, (((0,), (0,)), ((), ())), preferred_element_type=f32)


def place(parts, starts, out_shape, puts):
    count = len(puts)

    def kernel(starts_ref, *refs):
        ins, out, held, sems_in, sems_out = refs[: len(parts)], *refs[len(parts) :]
        arriving, leaving = [], []
        for n, (part, which, where) in enumerate(puts):
            arriving.append(pltpu.make_async_copy(ins[part], where(held, starts_ref[which]), sems_in.at[n]))
            arriving[-1].start()
        for n, (part, which, where) in enumerate(puts):
            start = starts_ref[which]
            arriving[n].wait()
            leaving.append(pltpu.make_async_copy(where(held, start), where(out, start), sems_out.at[n]))
            leaving[-1].start()
        for copy in leaving:
            copy.wait()

    size = sum(p.size * p.dtype.itemsize for p in parts)
    return pl.pallas_call(
        kernel,
        grid_spec=pltpu.PrefetchScalarGridSpec(
            num_scalar_prefetch=1,
            grid=(1,),
            in_specs=[pl.BlockSpec(memory_space=pl.ANY)] * len(parts),
            out_specs=pl.BlockSpec(memory_space=pl.ANY),
            scratch_shapes=[
                pltpu.VMEM(out_shape.shape, out_shape.dtype),
                pltpu.SemaphoreType.DMA((count,)),
                pltpu.SemaphoreType.DMA((count,)),
            ],
        ),
        out_shape=out_shape,
        compiler_params=params(),
        cost_estimate=cost(0, 2 * size),
    )(starts, *parts)


def attention_forward(qkv, lengths):
    seqs, slots, three = qkv.shape
    pairs = three // (3 * PAIR)

    def kernel(len_ref, qkv_ref, out_ref, lse_ref):
        valid_count = len_ref[pl.program_id(0)]
        q2 = qkv_ref[0, :, 0:PAIR]
        k2 = qkv_ref[0, :, PAIR : 2 * PAIR]
        vt = qkv_ref[0, :, 2 * PAIR : 3 * PAIR].T
        lane = lax.broadcasted_iota(jnp.int32, (slots, PAIR), 1)
        row = lax.broadcasted_iota(jnp.int32, (slots, slots), 0)
        halves = []
        for h in range(2):
            qh = jnp.where((lane < HEAD_DIM) == (h == 0), q2, jnp.zeros_like(q2))
            st = mm_nt(k2, qh) * (SCALE * LOG2E)
            st = jnp.where(row < valid_count, st, -1e30)
            top = jnp.max(st, axis=0, keepdims=True)
            p = jnp.exp2(st - top)
            total = jnp.sum(p, axis=0, keepdims=True)
            p_low = (p * (1.0 / total)).astype(bf16)
            halves.append(mm(vt[h * HEAD_DIM : (h + 1) * HEAD_DIM, :], p_low))
            lse_ref[0, 0, h : h + 1, :] = top + jnp.log2(total)
        out_ref[0] = jnp.concatenate(halves, axis=0).T.astype(bf16)

    grid_spec = pltpu.PrefetchScalarGridSpec(
        num_scalar_prefetch=1,
        grid=(seqs, pairs),
        in_specs=[pl.BlockSpec((1, slots, 3 * PAIR), lambda s, j, n: (s, 0, j))],
        out_specs=[
            pl.BlockSpec((1, slots, PAIR), lambda s, j, n: (s, 0, j)),
            pl.BlockSpec((1, 1, 2, slots), lambda s, j, n: (s, j, 0, 0)),
        ],
    )
    work = seqs * pairs * 2 * slots * slots
    return pl.pallas_call(
        kernel,
        grid_spec=grid_spec,
        out_shape=[
            jax.ShapeDtypeStruct((seqs, slots, pairs * PAIR), bf16),
            jax.ShapeDtypeStruct((seqs, pairs, 2, slots), f32),
        ],
        compiler_params=params(),
        cost_estimate=cost(work * 4 * PAIR * 2, qkv.size * 2.7, work),
    )(lengths, qkv)


def attention_backward(qkv, grad_heads, lse, lengths, seq, waits=()):
    _, slots, three = qkv.shape
    pairs = three // (3 * PAIR)

    def kernel(len_ref, qkv_ref, gh_ref, lse_ref, *refs):
        out_ref, sums_ref = refs[-2:]
        valid_count = len_ref[seq]
        q2 = qkv_ref[0, :, 0:PAIR]
        k2 = qkv_ref[0, :, PAIR : 2 * PAIR]
        v2 = qkv_ref[0, :, 2 * PAIR : 3 * PAIR]
        g2 = gh_ref[...]
        kt = k2.T
        lane = lax.broadcasted_iota(jnp.int32, (slots, PAIR), 1)
        row = lax.broadcasted_iota(jnp.int32, (slots, slots), 0)
        grad_k, grad_v, grad_q = [], [], []
        for h in range(2):
            mine = (lane < HEAD_DIM) == (h == 0)
            qh = jnp.where(mine, q2, jnp.zeros_like(q2))
            gh = jnp.where(mine, g2, jnp.zeros_like(g2))
            st = mm_nt(k2, qh) * (SCALE * LOG2E)
            p = jnp.exp2(st - lse_ref[0, 0, h : h + 1, :])
            p = jnp.where(row < valid_count, p, 0.0)
            dp = mm_nt(v2, gh)
            inner_sum = jnp.sum(p * dp, axis=0, keepdims=True)
            ds = (p * (dp - inner_sum)).astype(bf16)
            grad_v.append(mm(p.astype(bf16), g2))
            grad_k.append(mm(ds, q2))
            grad_q.append(mm(kt[h * HEAD_DIM : (h + 1) * HEAD_DIM, :], ds))
        gq = (jnp.concatenate(grad_q, axis=0).T * SCALE).astype(bf16)
        gk = (jnp.where(lane < HEAD_DIM, grad_k[0], grad_k[1]) * SCALE).astype(bf16)
        gv = jnp.where(lane < HEAD_DIM, grad_v[0], grad_v[1]).astype(bf16)
        out_ref[:, 0:PAIR] = gq
        out_ref[:, PAIR : 2 * PAIR] = gk
        out_ref[:, 2 * PAIR : 3 * PAIR] = gv
        sums_ref[0, 0:1, :] = jnp.sum(gq.astype(f32), axis=0, keepdims=True)
        sums_ref[0, 1:2, :] = jnp.sum(gv.astype(f32), axis=0, keepdims=True)

    grid_spec = pltpu.PrefetchScalarGridSpec(
        num_scalar_prefetch=1,
        grid=(pairs,),
        in_specs=[
            pl.BlockSpec((1, slots, 3 * PAIR), lambda j, n: (seq, 0, j)),
            pl.BlockSpec((slots, PAIR), lambda j, n: (seq, j)),
            pl.BlockSpec((1, 1, 2, slots), lambda j, n: (seq, j, 0, 0)),
        ]
        + [ANY] * len(waits),
        out_specs=[
            pl.BlockSpec((slots, 3 * PAIR), lambda j, n: (0, j)),
            pl.BlockSpec((1, 2, PAIR), lambda j, n: (j, 0, 0)),
        ],
    )
    work = pairs * 2 * slots * slots
    return pl.pallas_call(
        kernel,
        grid_spec=grid_spec,
        out_shape=[
            jax.ShapeDtypeStruct((slots, three), bf16),
            jax.ShapeDtypeStruct((pairs, 2, PAIR), f32),
        ],
        compiler_params=params(),
        cost_estimate=cost(work * 10 * PAIR * 2, slots * three * 5, work),
    )(lengths, qkv, grad_heads, lse, *waits)


def project(x, w, bias, waits=(), cols=768):
    rows, depth = x.shape
    width = bias.shape[1]

    def kernel(x_ref, w_ref, b_ref, *refs):
        refs[-1][...] = (mm(x_ref[...], w_ref[...]) + b_ref[...]).astype(bf16)

    return pl.pallas_call(
        kernel,
        grid=(width // cols,),
        in_specs=[
            pl.BlockSpec((rows, depth), lambda j: (0, 0)),
            pl.BlockSpec((depth, cols), lambda j: (0, j)),
            pl.BlockSpec((1, cols), lambda j: (0, j)),
        ]
        + [ANY] * len(waits),
        out_specs=pl.BlockSpec((rows, cols), lambda j: (0, j)),
        out_shape=jax.ShapeDtypeStruct((rows, width), bf16),
        compiler_params=params(),
        cost_estimate=cost(2 * rows * depth * width, 2 * (x.size + depth * width + rows * width)),
    )(x, w, bias, *waits)


def normed(summed):
    centred = summed - jnp.mean(summed, axis=-1, keepdims=True)
    rstd = lax.rsqrt(jnp.mean(centred * centred, axis=-1, keepdims=True) + EPS)
    return centred * rstd, rstd


def norm_back(grad_hat, hat, rstd):
    return rstd * (
        grad_hat
        - jnp.mean(grad_hat, axis=-1, keepdims=True)
        - hat * jnp.mean(grad_hat * hat, axis=-1, keepdims=True)
    )


def joined(w_ref, c, cols=slice(None)):
    part = w_ref[:, c, :, cols]
    return part.reshape(part.shape[0] * part.shape[1], part.shape[2])


def reordered(ref, features, first=0, count=8, block=128):
    parts = []
    for k in range(first, first + count):
        start = pl.multiple_of(features[k] * block, block)
        parts.append(ref[:, pl.ds(start, block)].T)
    return jnp.concatenate(parts, axis=0)


def out_forward(heads, w_mid, x, b_out, gain, shift, features, rows=256):
    total, width = x.shape
    blocks, ctx, depth, _ = w_mid.shape
    cols = width // ctx

    def kernel(feat_ref, h_ref, w_ref, x_ref, b_ref, g_ref, s_ref, hat_ref, rstd_ref, low_ref, turned_ref):
        h = h_ref[...]
        attended = jnp.concatenate([mm(h, joined(w_ref, c)) for c in range(ctx)], axis=1)
        summed = attended + b_ref[...] + x_ref[...].astype(f32)
        hat, rstd = normed(summed)
        hat_ref[...] = hat
        rstd_ref[...] = rstd
        low_ref[...] = (hat * g_ref[...] + s_ref[...]).astype(bf16)
        turned_ref[...] = reordered(low_ref, feat_ref)

    block = pl.BlockSpec((rows, width), lambda i, f: (i, 0))
    vec = pl.BlockSpec((1, width), lambda i, f: (0, 0))
    weight = pl.BlockSpec((blocks, ctx, depth, cols), lambda i, f: (0, 0, 0, 4))
    grid_spec = pltpu.PrefetchScalarGridSpec(
        num_scalar_prefetch=1,
        grid=(total // rows,),
        in_specs=[block, weight, block, vec, vec, vec],
        out_specs=[
            block,
            pl.BlockSpec((rows, 1), lambda i, f: (i, 0)),
            block,
            pl.BlockSpec((width, rows), lambda i, f: (0, i)),
        ],
    )
    return pl.pallas_call(
        kernel,
        grid_spec=grid_spec,
        out_shape=[
            jax.ShapeDtypeStruct((total, width), f32),
            jax.ShapeDtypeStruct((total, 1), f32),
            jax.ShapeDtypeStruct((total, width), bf16),
            jax.ShapeDtypeStruct((width, total), bf16),
        ],
        compiler_params=params(),
        cost_estimate=cost(2 * total * width * width, total * width * 12 + width * width * 2),
    )(features, heads, w_mid, x, b_out, gain, shift)


def gelu_pair(x):
    density = jnp.exp2(x * x * (-0.5 * LOG2E))
    t = 1.0 / (jnp.abs(x) * (0.3275911 * 0.7071067811865476) + 1.0)
    poly = 1.061405429 * 0.5
    for coefficient in (-1.453152027, 1.421413741, -0.284496736, 0.254829592):
        poly = poly * t + coefficient * 0.5
    tail = poly * t * density
    phi = jnp.where(x < 0, tail, 1.0 - tail)
    active = x * phi
    slope = phi + x * density * 0.3989422804014327
    return active, slope


def ffn_one(hidden, w_mid, b_inner, cols=1024, chunk=256):
    rows, depth = hidden.shape
    width = b_inner.shape[1]
    blocks, ctx, deep, _ = w_mid.shape
    per = width // ctx // cols

    def kernel(h_ref, w_ref, b_ref, act_ref, slope_ref):
        w = joined(w_ref, 0)
        for c in range(rows // chunk):
            part = pl.ds(c * chunk, chunk)
            inner = mm(h_ref[part, :], w) + b_ref[...]
            active, slope = gelu_pair(inner)
            act_ref[part, :] = active.astype(bf16)
            slope_ref[part, :] = slope.astype(bf16)

    out = pl.BlockSpec((rows, cols), lambda j: (0, j))
    return pl.pallas_call(
        kernel,
        grid=(width // cols,),
        in_specs=[
            pl.BlockSpec((rows, depth), lambda j: (0, 0)),
            pl.BlockSpec((blocks, 1, deep, cols), lambda j: (0, j // per, 0, j % per)),
            pl.BlockSpec((1, cols), lambda j: (0, j)),
        ],
        out_specs=[out, out],
        out_shape=[jax.ShapeDtypeStruct((rows, width), bf16)] * 2,
        compiler_params=params(),
        cost_estimate=cost(2 * rows * depth * width, 2 * (hidden.size + depth * width + 2 * rows * width), 2 * rows * width),
    )(hidden, w_mid, b_inner)


def ffn_two(active, w_outer, hat_one, cot, lengths, vectors, slots, rows=256):
    total, depth = active.shape
    width = hat_one.shape[1]
    ctx = w_outer.shape[1]
    per_seq = slots // rows

    def kernel(len_ref, a_ref, w_ref, hat_ref, cot_ref, vec_ref, mixed_ref, grad_ref, low_ref, sums_ref):
        i = pl.program_id(0)
        g_one, s_one, b_outer, g_two, s_two = (vec_ref[k : k + 1, :] for k in range(5))
        a = a_ref[...]
        outer = jnp.concatenate([mm(a, joined(w_ref, c)) for c in range(ctx)], axis=1)
        summed = outer + b_outer + (hat_ref[...] * g_one + s_one)
        hat, rstd = normed(summed)
        mixed_ref[...] = (hat * g_two + s_two).astype(bf16)
        slot = (i % per_seq) * rows + lax.broadcasted_iota(jnp.int32, (rows, width), 0)
        grad_y = jnp.where(slot < len_ref[i // per_seq], cot_ref[...].astype(f32), 0.0)
        grad = norm_back(grad_y * g_two, hat, rstd)
        grad_ref[...] = grad
        low = grad.astype(bf16)
        low_ref[...] = low

        @pl.when(i == 0)
        def _():
            sums_ref[...] = jnp.zeros_like(sums_ref)

        sums_ref[0:1, :] += jnp.sum(grad_y * hat, axis=0, keepdims=True)
        sums_ref[1:2, :] += jnp.sum(grad_y, axis=0, keepdims=True)
        sums_ref[2:3, :] += jnp.sum(low.astype(f32), axis=0, keepdims=True)

    block = pl.BlockSpec((rows, width), lambda i, n: (i, 0))
    grid_spec = pltpu.PrefetchScalarGridSpec(
        num_scalar_prefetch=1,
        grid=(total // rows,),
        in_specs=[
            pl.BlockSpec((rows, depth), lambda i, n: (i, 0)),
            pl.BlockSpec(w_outer.shape, lambda i, n: (0, 0, 0, 0)),
            block,
            block,
            pl.BlockSpec((8, width), lambda i, n: (0, 0)),
        ],
        out_specs=[block, block, block, pl.BlockSpec((8, width), lambda i, n: (0, 0))],
    )
    return pl.pallas_call(
        kernel,
        grid_spec=grid_spec,
        out_shape=[
            jax.ShapeDtypeStruct((total, width), bf16),
            jax.ShapeDtypeStruct((total, width), f32),
            jax.ShapeDtypeStruct((total, width), bf16),
            jax.ShapeDtypeStruct((8, width), f32),
        ],
        compiler_params=params(),
        cost_estimate=cost(2 * total * width * depth, active.size * 2 + w_outer.size * 2 + total * width * 14),
    )(lengths, active, w_outer, hat_one, cot, vectors)


def ffn_back(grad_low, start, hidden_t, active, slope, w_outer, w_mid, order, waits=(), cols=512):
    rows, width = grad_low.shape
    count = order.shape[0]
    half = width // 2
    blocks, ctx, deep, _ = w_mid.shape
    per = active.shape[1] // ctx // cols
    outer_rows = w_outer.shape[2]
    outer_cols = w_outer.shape[3]

    def kernel(ord_ref, g_ref, start_ref, ht_ref, a_ref, s_ref, wo_ref, wi_ref, *refs):
        grad_ref, dwo_ref, dws_ref, dwk_ref, bias_ref = refs[-5:]
        j = pl.program_id(0)
        grad = g_ref[...]
        grad_active = sum(
            mm_nt(grad[:, c * outer_cols : (c + 1) * outer_cols], joined(wo_ref, c)) for c in range(ctx)
        )
        inner = (grad_active * s_ref[...].astype(f32)).astype(bf16)
        bias_ref[...] = jnp.sum(inner.astype(f32), axis=0, keepdims=True)
        dwo_ref[...] = mm_tn(a_ref[...], grad).astype(bf16)
        dws_ref[...] = mm(ht_ref[0:half, :], inner).astype(bf16)
        dwk_ref[...] = mm(ht_ref[half:width, :], inner).astype(bf16)

        @pl.when(j == 0)
        def _():
            grad_ref[...] = start_ref[...]

        grad_ref[...] += mm_nt(inner, joined(wi_ref, 0))

    whole = lambda j, o: (0, 0)
    grid_spec = pltpu.PrefetchScalarGridSpec(
        num_scalar_prefetch=1,
        grid=(count,),
        in_specs=[
            pl.BlockSpec((rows, width), whole),
            pl.BlockSpec((rows, width), whole),
            pl.BlockSpec((width, rows), whole),
            pl.BlockSpec((rows, cols), lambda j, o: (0, o[j])),
            pl.BlockSpec((rows, cols), lambda j, o: (0, o[j])),
            pl.BlockSpec((cols // outer_rows, ctx, outer_rows, outer_cols), lambda j, o: (o[j], 0, 0, 0)),
            pl.BlockSpec((blocks, 1, deep, cols), lambda j, o: (0, o[j] // per, 0, o[j] % per)),
        ]
        + [ANY] * len(waits),
        out_specs=[
            pl.BlockSpec((rows, width), whole),
            pl.BlockSpec((cols, width), lambda j, o: (j, 0)),
            pl.BlockSpec((half, cols), lambda j, o: (0, j)),
            pl.BlockSpec((half, cols), lambda j, o: (0, j)),
            pl.BlockSpec((1, cols), lambda j, o: (0, j)),
        ],
    )
    return pl.pallas_call(
        kernel,
        grid_spec=grid_spec,
        out_shape=[
            jax.ShapeDtypeStruct((rows, width), f32),
            jax.ShapeDtypeStruct((count * cols, width), bf16),
            jax.ShapeDtypeStruct((half, count * cols), bf16),
            jax.ShapeDtypeStruct((half, count * cols), bf16),
            jax.ShapeDtypeStruct((1, count * cols), f32),
        ],
        compiler_params=params(),
        cost_estimate=cost(8 * rows * width * count * cols, 12 * count * cols * width + 12 * rows * width),
    )(order, grad_low, start, hidden_t, active, slope, w_outer, w_mid, *waits)


def out_back(grad_hidden, hat, rstd, gain, w_mid, heads, features, waits=(), rows=256):
    total, width = grad_hidden.shape
    half = width // 2
    steps = total // rows
    blocks, ctx, depth, _ = w_mid.shape
    cols = width // ctx

    def kernel(feat_ref, gh_ref, hat_ref, rstd_ref, gain_ref, w_ref, h_ref, *refs):
        one_ref, heads_ref, dws_ref, dwk_ref, sums_ref, acc = refs[-6:]
        i = pl.program_id(0)
        grad_y = gh_ref[...]
        hat = hat_ref[...]
        grad = norm_back(grad_y * gain_ref[...], hat, rstd_ref[...])
        one_ref[...] = grad
        low = grad.astype(bf16)
        heads_ref[...] = sum(mm_nt(low[:, c * cols : (c + 1) * cols], joined(w_ref, c)) for c in range(ctx)).astype(bf16)

        @pl.when(i == 0)
        def _():
            sums_ref[...] = jnp.zeros_like(sums_ref)
            acc[...] = jnp.zeros_like(acc)

        acc[...] += mm(reordered(h_ref, feat_ref), low)
        sums_ref[0:1, :] += jnp.sum(grad_y * hat, axis=0, keepdims=True)
        sums_ref[1:2, :] += jnp.sum(grad_y, axis=0, keepdims=True)
        sums_ref[2:3, :] += jnp.sum(low.astype(f32), axis=0, keepdims=True)

        @pl.when(i == steps - 1)
        def _():
            dws_ref[...] = acc[0:half, :].astype(bf16)
            dwk_ref[...] = acc[half:width, :].astype(bf16)

    block = pl.BlockSpec((rows, width), lambda i, f: (i, 0))
    whole = lambda i, f: (0, 0)
    grid_spec = pltpu.PrefetchScalarGridSpec(
        num_scalar_prefetch=1,
        grid=(steps,),
        in_specs=[
            block,
            block,
            pl.BlockSpec((rows, 1), lambda i, f: (i, 0)),
            pl.BlockSpec((1, width), whole),
            pl.BlockSpec((blocks, ctx, depth, cols), lambda i, f: (0, 0, 0, 4)),
            block,
        ]
        + [ANY] * len(waits),
        out_specs=[
            block,
            block,
            pl.BlockSpec((half, width), whole),
            pl.BlockSpec((half, width), whole),
            pl.BlockSpec((8, width), whole),
        ],
        scratch_shapes=[pltpu.VMEM((width, width), f32)],
    )
    return pl.pallas_call(
        kernel,
        grid_spec=grid_spec,
        out_shape=[
            jax.ShapeDtypeStruct((total, width), f32),
            jax.ShapeDtypeStruct((total, width), bf16),
            jax.ShapeDtypeStruct((half, width), bf16),
            jax.ShapeDtypeStruct((half, width), bf16),
            jax.ShapeDtypeStruct((8, width), f32),
        ],
        compiler_params=params(),
        cost_estimate=cost(4 * total * width * width, total * width * 16 + width * width * 4),
    )(features, grad_hidden, hat, rstd, gain, w_mid, heads, *waits)


def attn_weight_grads(x, grads, features, part, got=None, waits=(), cols=768):
    total, width = x.shape
    count = len(grads)
    slots, three = grads[0].shape
    half = width // 2
    blocks = half // 128

    def kernel(feat_ref, x_ref, *refs):
        out_ref, turned = refs[-2:]

        @pl.when(pl.program_id(0) == 0)
        def _():
            turned[...] = reordered(x_ref, feat_ref, part * blocks, blocks)

        value = sum(mm(turned[:, n * slots : (n + 1) * slots], refs[n][...]) for n in range(count))
        if got is not None:
            value = value + refs[count][...].astype(f32)
        out_ref[...] = value.astype(bf16)

    column = pl.BlockSpec((slots, cols), lambda j, f: (0, j))
    out = pl.BlockSpec((half, cols), lambda j, f: (0, j))
    extra = [] if got is None else [got]
    grid_spec = pltpu.PrefetchScalarGridSpec(
        num_scalar_prefetch=1,
        grid=(three // cols,),
        in_specs=[pl.BlockSpec((total, width), lambda j, f: (0, 0))]
        + [column] * count
        + [out] * len(extra)
        + [ANY] * len(waits),
        out_specs=out,
        scratch_shapes=[pltpu.VMEM((half, total), bf16)],
    )
    return pl.pallas_call(
        kernel,
        grid_spec=grid_spec,
        out_shape=jax.ShapeDtypeStruct((half, three), bf16),
        compiler_params=params(),
        cost_estimate=cost(total * width * three, 2 * (total * width + total * three + width * three)),
    )(features, x, *grads, *extra, *waits)


def token_grads(grad_qkv, w_attn, grad_one, seq, waits=(), rows=256):
    slots, three = grad_qkv.shape
    width = grad_one.shape[1]
    steps = slots // rows

    def kernel(g_ref, w_ref, one_ref, *refs):
        refs[-1][...] = (mm_nt(g_ref[...], w_ref[...]) + one_ref[...]).astype(bf16)

    return pl.pallas_call(
        kernel,
        grid=(steps,),
        in_specs=[
            pl.BlockSpec((rows, three), lambda i: (i, 0)),
            pl.BlockSpec((width, three), lambda i: (0, 0)),
            pl.BlockSpec((rows, width), lambda i: (seq * steps + i, 0)),
        ]
        + [ANY] * len(waits),
        out_specs=pl.BlockSpec((rows, width), lambda i: (i, 0)),
        out_shape=jax.ShapeDtypeStruct((slots, width), bf16),
        compiler_params=params(),
        cost_estimate=cost(2 * slots * three * width, 2 * (slots * three + width * three) + slots * width * 6),
    )(grad_qkv, w_attn, grad_one, *waits)


def swap(array, axis, size, mask):
    return lax.ppermute(array, axis, [(i, i ^ mask) for i in range(size)])


def shift(array, axis, size, by):
    return lax.ppermute(array, axis, [(i, (i + by) % size) for i in range(size)])


def after(array, *earlier):
    return lax.optimization_barrier((array, *earlier))[0]


def after_all(array, earlier):
    return after(array, *earlier) if earlier else array


class Columns:
    def __init__(self, shard, c):
        self.c, self.shard = c, shard

    def first(self):
        self.near = swap(self.shard, "ctx", 4, 1)
        return self.near

    def second(self):
        odd = (self.c & 1) == 1
        self.pair = jnp.stack(
            [jnp.where(odd, self.near, self.shard), jnp.where(odd, self.shard, self.near)]
        )
        self.across = lax.ppermute(self.pair, "ctx", [(1, 2), (2, 1)])
        return self.across

    def third(self):
        self.outwards = lax.ppermute(self.across, "ctx", [(1, 0), (2, 3)])
        return self.outwards

    def pieces(self):
        middle = (self.c == 1) | (self.c == 2)
        other = jnp.where(middle, self.across, self.outwards)
        upper = self.c >= 2
        return jnp.concatenate([jnp.where(upper, other, self.pair), jnp.where(upper, self.pair, other)])


def gather_rows(block, r, dp):
    if dp != 8:
        return lax.all_gather(block, "dp", axis=0, tiled=True), ()
    rows, width = block.shape
    half = rows // 2
    by_x = swap(block, "dp", dp, 2)
    by_y = swap(block, "dp", dp, 4)
    far_top = swap(by_x[:half], "dp", dp, 4)
    far_low = swap(by_y[half:], "dp", dp, 2)
    own = [block, by_x, by_y, far_top, far_low]
    twin = [swap(part, "dp", dp, 1) for part in own]

    def at(offset, count):
        return lambda out, start: out.at[pl.ds(pl.multiple_of(start + offset, half), count), :]

    puts = []
    for n, base in ((0, 0), (5, 1)):
        puts += [
            (n, base, at(0, rows)),
            (n + 1, base ^ 2, at(0, rows)),
            (n + 2, base ^ 4, at(0, rows)),
            (n + 3, base ^ 6, at(0, half)),
            (n + 4, base ^ 6, at(half, half)),
        ]
    starts = jnp.stack([(r ^ m) * rows for m in range(8)]).astype(jnp.int32)
    shape = jax.ShapeDtypeStruct((dp * rows, width), block.dtype)
    return place(own + twin, starts, shape, puts), (by_x, by_y)


class Exchange:
    def __init__(self, array, c, ctx, gather):
        self.c, self.ctx, self.gather = c, ctx, gather
        if gather:
            seqs, self.count, self.width = array.shape
            self.per = seqs // ctx
        else:
            self.per, total, self.width = array.shape
            self.count = total // ctx
        self.dtype = array.dtype
        self.parts = [self.piece(array, (c + d) % ctx) for d in range(ctx)]
        self.pieces = tuple(self.parts)

    def piece(self, array, index):
        start = (index * self.per, 0, 0) if self.gather else (0, index * self.count, 0)
        return lax.dynamic_slice(array, start, (self.per, self.count, self.width))

    def send(self, *which):
        for d in which or range(1, self.ctx):
            self.parts[d] = shift(self.parts[d], "ctx", self.ctx, d)
        return self.parts

    def arrive(self, *earlier):
        self.parts = list(lax.optimization_barrier((*self.parts, *earlier))[: self.ctx])

    def placed(self):
        step = self.count if self.gather else self.per
        starts = jnp.stack([((self.c - d) % self.ctx) * step for d in range(self.ctx)]).astype(jnp.int32)
        if self.gather:
            at = lambda out, start: out.at[:, pl.ds(pl.multiple_of(start, step), step), :]
            shape = (self.per, self.ctx * self.count, self.width)
        else:
            at = lambda out, start: out.at[pl.ds(start, step), :, :]
            shape = (self.per * self.ctx, self.count, self.width)
        return place(self.parts, starts, jax.ShapeDtypeStruct(shape, self.dtype), [(d, d, at) for d in range(self.ctx)])


class RowSum:
    def __init__(self, parts, r, dp):
        self.parts, self.dp = parts, dp
        self.y, self.x = (r >> 2) & 1, (r >> 1) & 1
        self.widths = [kept.shape[-1] for _, kept in parts]

    def pick(self, array, yi, xi, h):
        _, rows, width = array.shape
        array = array.reshape(2, 2, 2, rows // 2, width)
        start = (0 if yi is None else yi, 0 if xi is None else xi, h, 0, 0)
        sizes = (2 if yi is None else 1, 2 if xi is None else 1, 1, rows // 2, width)
        out = lax.dynamic_slice(array, tuple(jnp.int32(s) for s in start), sizes)
        return out.reshape(sizes[0] * sizes[1], rows // 2, width).astype(f32)

    def summed(self, yi, xi, h):
        return [
            self.pick(kept, yi, xi, h) if got is None else self.pick(got, yi, xi, h) + self.pick(kept, yi, xi, h)
            for got, kept in self.parts
        ]

    def pack(self, arrays):
        return jnp.concatenate([a.astype(bf16) for a in arrays], axis=-1)

    def plus(self, arrays, packed, index=None):
        if index is not None:
            packed = lax.dynamic_slice_in_dim(packed, index, 1, axis=0)
        out, at = [], 0
        for array, width in zip(arrays, self.widths):
            out.append(array + lax.slice_in_dim(packed, at, at + width, axis=2).astype(f32))
            at += width
        return out

    def first_sends(self):
        self.sends = (self.pack(self.summed(None, 1 - self.x, 0)), self.pack(self.summed(1 - self.y, None, 1)))
        return self.sends

    def first(self):
        self.got_x = swap(self.sends[0], "dp", self.dp, 2)
        self.got_y = swap(self.sends[1], "dp", self.dp, 4)
        return (self.got_x, self.got_y)

    def first_there(self, *earlier):
        self.got_x, self.got_y = lax.optimization_barrier((self.got_x, self.got_y, *earlier))[:2]

    def second_there(self, *earlier):
        self.top, self.low = lax.optimization_barrier((self.top, self.low, *earlier))[:2]

    def second_sends(self):
        y, x = self.y, self.x
        self.sends = (
            self.pack(self.plus(self.summed(1 - y, x, 0), self.got_x, 1 - y)),
            self.pack(self.plus(self.summed(y, 1 - x, 1), self.got_y, 1 - x)),
        )
        return self.sends

    def second(self):
        self.top = swap(self.sends[0], "dp", self.dp, 4)
        self.low = swap(self.sends[1], "dp", self.dp, 2)
        return (self.top, self.low)

    def result(self):
        y, x = self.y, self.x
        top = self.plus(self.plus(self.summed(y, x, 0), self.got_x, y), self.top)
        low = self.plus(self.plus(self.summed(y, x, 1), self.got_y, x), self.low)
        return [jnp.concatenate([a[0], b[0]], axis=0) for a, b in zip(top, low)]


class ColumnSum:
    def __init__(self, blocks, c):
        self.blocks, self.c = blocks, c
        self.sizes = [b.shape[1] // 4 for b in blocks]
        self.pair, self.odd = c >> 1, c & 1

    def pack(self, arrays):
        return jnp.concatenate([a.astype(bf16) for a in arrays], axis=1)

    def unpack(self, array, times):
        pieces, at = [], 0
        for size in self.sizes:
            pieces.append(array[:, at : at + times * size].astype(f32))
            at += times * size
        return pieces

    def columns(self, arrays, index, times):
        return [
            lax.dynamic_slice_in_dim(a, index * times * s, times * s, axis=1) for a, s in zip(arrays, self.sizes)
        ]

    def first_send(self):
        self.other = self.columns(self.blocks, 1 - self.pair, 2)
        self.send = self.pack(self.other)
        return self.send

    def first(self):
        self.got = lax.ppermute(self.send, "ctx", [(0, 1), (3, 2)])
        return self.got

    def there(self, *earlier):
        self.got = after(self.got, *earlier)

    def second_send(self):
        self.send = self.pack([a + b for a, b in zip(self.other, self.unpack(self.got, 2))])
        return self.send

    def second(self):
        self.got = lax.ppermute(self.send, "ctx", [(1, 2), (2, 1)])
        return self.got

    def third_send(self):
        mine = self.columns(self.blocks, self.pair, 2)
        self.mine = [a + b for a, b in zip(mine, self.unpack(self.got, 2))]
        self.send = self.pack(self.columns(self.mine, 1 - self.odd, 1))
        return self.send

    def third(self):
        self.got = swap(self.send, "ctx", 4, 1)
        return self.got

    def result(self):
        return [a + b for a, b in zip(self.columns(self.mine, self.odd, 1), self.unpack(self.got, 1))]

    def whole(self):
        for stage in ("first", "second", "third"):
            getattr(self, stage + "_send")()
            getattr(self, stage)()
        return self.result()


def pair_columns(query, key, value):
    rows, width = query.shape
    pieces = []
    for j in range(width // PAIR):
        pieces += [a[:, j * PAIR : (j + 1) * PAIR] for a in (query, key, value)]
    return jnp.concatenate(pieces, axis=1)


def on_device(
    dp,
    ctx,
    tokens,
    lengths,
    cotangent,
    weight_query,
    weight_key,
    weight_value,
    weight_out,
    weight_inner,
    weight_outer,
    bias_query,
    bias_value,
    bias_out,
    bias_inner,
    bias_outer,
    gain_attn,
    shift_attn,
    gain_ffn,
    shift_ffn,
):
    seq_total, slot_count, width = tokens.shape
    units = bias_inner.shape[0]
    per = seq_total // ctx
    slots = slot_count * ctx
    rows = per * slots
    c = lax.axis_index("ctx")
    r = lax.axis_index("dp")
    core = r & 1
    paired = dp == 8

    own_lengths = lax.dynamic_slice(lengths, (c * per,), (per,))
    attn_shard = pair_columns(weight_query, weight_key, weight_value)
    attn = Columns(attn_shard, c)
    mid = Columns(jnp.concatenate([weight_inner, weight_out], axis=1), c)
    outer = Columns(weight_outer, c)
    attn.first()
    mid.shard = after(mid.shard, attn.near)
    attn.second()
    mid.first()
    attn.across, mid.near, outer.shard = lax.optimization_barrier((attn.across, mid.near, outer.shard))
    attn.third()
    mid.second()
    outer.first()
    attn.outwards, mid.across, outer.near, tokens = lax.optimization_barrier(
        (attn.outwards, mid.across, outer.near, tokens)
    )
    mid.third()
    outer.second()
    x = Exchange(tokens, c, ctx, True)
    x.send(2)
    block = jnp.concatenate([p for p in attn.pieces()], axis=1)
    w_attn, early = gather_rows(block, r, dp)
    x.parts[1], x.parts[3], mid.outwards, outer.across = lax.optimization_barrier(
        (x.parts[1], x.parts[3], mid.outwards, outer.across)
    )
    x.send(1, 3)
    w_mid = lax.all_gather(after_all(mid.pieces(), early), "dp", axis=0)
    outer.across = after(outer.across, x.parts[2])
    outer.third()
    x.arrive(outer.outwards)
    x = x.placed().reshape(rows, width)
    cot = Exchange(after(cotangent, x), c, ctx, True)
    cot.send()

    if paired:
        order_s = (jnp.arange(4) * 2 + (1 - core)).astype(jnp.int32)
        order_k = (jnp.arange(4) * 2 + core).astype(jnp.int32)
    else:
        order_s, order_k = jnp.arange(4, dtype=jnp.int32), jnp.arange(4, 8, dtype=jnp.int32)
    features = jnp.concatenate([order_s, order_k])

    bias_qkv = pair_columns(bias_query[None], jnp.zeros_like(bias_query)[None], bias_value[None])
    qkv = project(x, w_attn, bias_qkv, cot.pieces).reshape(per, slots, 3 * width)
    outer.outwards = after(outer.outwards, qkv)
    w_outer = lax.all_gather(outer.pieces(), "dp", axis=0)
    heads, lse = attention_forward(qkv, own_lengths)
    heads = heads.reshape(rows, width)
    hat_one, rstd_one, hidden_low, hidden_t = out_forward(
        heads, w_mid, x, bias_out[None], gain_attn[None], shift_attn[None], features
    )
    active, slope = ffn_one(hidden_low, w_mid, bias_inner[None])
    cot.arrive(hidden_low)
    cot = cot.placed().reshape(rows, width)
    vectors = jnp.stack([gain_attn, shift_attn, bias_outer, gain_ffn, shift_ffn] + [shift_ffn] * 3)
    mixed, grad_two, grad_outer, sums_two = ffn_two(
        active, w_outer, hat_one, cot, own_lengths, vectors, slots
    )
    mixed = Exchange(mixed.reshape(per, slots, width), c, ctx, False)
    mixed.send()

    def from_twin(sent):
        return swap(sent, "dp", dp, 1) if paired else sent

    def part(got, kept):
        blocks = (4, kept.shape[0] // 4, kept.shape[1])
        return (got.reshape(blocks), kept.reshape(blocks))

    grad_hidden, outer_s, inner_s1, inner_k1, bias_1 = ffn_back(
        grad_outer, grad_two, hidden_t, active, slope, w_outer, w_mid, order_s, mixed.pieces
    )
    got_outer = from_twin(outer_s)
    grad_hidden, outer_k, inner_s2, inner_k2, bias_2 = ffn_back(
        grad_outer, grad_hidden, hidden_t, active, slope, w_outer, w_mid, order_k, (mixed.parts[3],)
    )
    got_inner_1, got_inner_2 = from_twin(inner_s2), from_twin(inner_s1)
    hold = (mixed.parts[1],)
    if paired:
        sum_c = RowSum([part(after(got_outer, outer_k), outer_k)], r, dp)
        hold = (*hold, *sum_c.first_sends())
        sum_c.first()
    grad_one, grad_heads, out_s, out_k, sums_one = out_back(
        grad_hidden, hat_one, rstd_one, gain_attn[None], w_mid, heads, features, waits=hold
    )
    got_out = from_twin(out_s)
    got_inner_1, got_inner_2, out_k = lax.optimization_barrier((got_inner_1, got_inner_2, out_k))
    mixed.arrive(out_k)
    mixed = mixed.placed()
    grad_qkv, sums_qkv, slot_grads = [], [], []
    last = per - 1
    hold = (mixed, got_inner_1, got_inner_2)
    for n in range(per):
        grad, sums = attention_backward(qkv, grad_heads, lse, own_lengths, n, waits=hold)
        grad_qkv.append(grad)
        sums_qkv.append(sums)
        hold = ()
        if paired and n == 0:
            got_out = after(got_out, grad)
            sum_b = RowSum([part(got_inner_1, inner_k1), part(got_inner_2, inner_k2), part(got_out, out_k)], r, dp)
            sum_c.first_there(grad)
            hold = (*sum_c.second_sends(), *sum_b.first_sends())
            sum_c.second()
            sum_b.first()
        if n < last:
            tokens_n = token_grads(grad, w_attn, grad_one, n, waits=hold)
            slot_grads.append(Exchange(tokens_n[None], c, ctx, False))
            hold = slot_grads[-1].pieces
            if paired and n == 0:
                sum_c.second_there(tokens_n)
                hold = (*hold, sum_c.top, sum_c.low)
            slot_grads[-1].send()
    hold = []
    for exchange in slot_grads:
        exchange.arrive(grad_qkv[last])
        hold.append(exchange.placed())
    slot_grads = list(hold)
    if paired:
        cols_c = ColumnSum(sum_c.result(), c)
        sum_b.first_there(grad_qkv[last])
        hold = [*hold, after(cols_c.first_send(), grad_qkv[last]), *sum_b.second_sends()]
        cols_c.first()
        sum_b.second()
    qkv_s = attn_weight_grads(x, grad_qkv, features, 0, waits=hold)
    got_qkv = from_twin(qkv_s)
    hold = []
    if paired:
        cols_c.there(qkv_s)
        hold.append(cols_c.second_send())
        cols_c.second()
    tokens_n = token_grads(grad_qkv[last], w_attn, grad_one, last, waits=hold)
    slots_n = Exchange(tokens_n[None], c, ctx, False)
    slots_n.send()
    if paired:
        sum_b.second_there(tokens_n)
        cols_b = ColumnSum(sum_b.result(), c)
        cols_c.there(tokens_n)
        hold = (cols_b.first_send(), cols_c.third_send(), *slots_n.pieces)
        cols_b.first()
        cols_c.third()
        qkv_k = attn_weight_grads(x, grad_qkv, features, 1, after(got_qkv, tokens_n), hold)
        sum_a = RowSum([(None, qkv_k.reshape(4, qkv_k.shape[0] // 4, qkv_k.shape[1]))], r, dp)
        cols_c.there(qkv_k)
        sends = sum_a.first_sends()
        sum_a.first()
        cols_b.there(*sends)
        cols_b.second_send()
        cols_b.second()
        (sum_outer,) = cols_c.result()
        slots_n.arrive(cols_b.send)
        sum_a.first_there(cols_b.send, *slots_n.parts)
        sends = sum_a.second_sends()
        sum_a.second()
        cols_b.there(*sends)
        cols_b.third_send()
        cols_b.third()
        slots_n.arrive(cols_b.send)
        sum_a.second_there(cols_b.send)
        cols_a = ColumnSum(sum_a.result(), c)
        cols_a.first_send()
        cols_a.first()
    else:
        qkv_k = attn_weight_grads(x, grad_qkv, features, 1)
    slot_grads.append(slots_n.placed())
    grad_tokens = jnp.stack(slot_grads, axis=1)
    grad_tokens = grad_tokens.reshape(seq_total, slot_count, width).astype(f32)

    if paired:
        cols_b.there(cols_a.send)
        inner_1, inner_2, sum_out = cols_b.result()
        cols_a.second_send()
        cols_a.second()
        cols_a.third_send()
        cols_a.third()
        (sum_qkv,) = cols_a.result()
        sum_inner = jnp.where(
            core == 0,
            jnp.concatenate([inner_2, inner_1], axis=1),
            jnp.concatenate([inner_1, inner_2], axis=1),
        )
        b_1, b_2 = bias_1.reshape(4, -1), bias_2.reshape(4, -1)
        bias_units = jnp.where(core == 0, jnp.stack([b_2, b_1], axis=1), jnp.stack([b_1, b_2], axis=1)).reshape(units)
    else:

        def over_dp(*arrays):
            array = jnp.concatenate(arrays, axis=0)
            return lax.psum_scatter(array.astype(f32), "dp", scatter_dimension=0, tiled=True)

        inner_s, inner_k = jnp.concatenate([inner_s1, inner_s2], axis=1), jnp.concatenate([inner_k1, inner_k2], axis=1)
        (sum_outer,) = ColumnSum([over_dp(outer_s, outer_k)], c).whole()
        sum_inner, sum_out = ColumnSum([over_dp(inner_s, inner_k), over_dp(out_s, out_k)], c).whole()
        (sum_qkv,) = ColumnSum([over_dp(qkv_s, qkv_k)], c).whole()
        bias_units = jnp.concatenate([bias_1[0], bias_2[0]])

    own_rows = sum_qkv.shape[0]
    sum_qkv = sum_qkv.reshape(own_rows, -1, 3, PAIR)
    sum_query, sum_key, sum_value = (sum_qkv[:, :, k].reshape(own_rows, -1) for k in range(3))

    sums_qkv = sum(sums_qkv)
    packed = jnp.concatenate(
        [
            sums_qkv[:, 0].reshape(-1),
            sums_qkv[:, 1].reshape(-1),
            sums_one[2],
            bias_units,
            sums_two[2],
            sums_one[0],
            sums_one[1],
            sums_two[0],
            sums_two[1],
        ]
    )
    packed = lax.all_gather(packed.reshape(-1, 128), ("dp", "ctx"))
    if paired:
        packed = after(packed, cols_a.send)
    packed = jnp.sum(packed, axis=0).reshape(-1)
    totals, at = [], 0
    for size in (width, width, width, units, width, width, width, width, width):
        totals.append(packed[at : at + size])
        at += size
    return (mixed, grad_tokens, sum_query, sum_key, sum_value, sum_out, sum_inner, sum_outer, *totals)


def solution(mesh):
    rows = P("dp", "ctx", None)
    matrix = P("dp", "ctx")
    in_specs = (rows, P("dp"), rows) + (matrix,) * 6 + (P(),) * 9
    out_specs = (rows, rows) + (matrix,) * 6 + (P(),) * 9
    step = functools.partial(on_device, mesh.shape["dp"], mesh.shape["ctx"])
    return jax.shard_map(step, mesh=mesh, in_specs=in_specs, out_specs=out_specs, check_vma=False)
```

```python
import functools

import jax
import jax.numpy as jnp
from jax import lax
from jax.experimental import pallas as pl
from jax.experimental.pallas import tpu as pltpu
from jax.sharding import PartitionSpec as P

HEAD_DIM = 64
PAIR = 128
EPS = 1e-05
SCALE = 0.125
LOG2E = 1.4426950408889634
VMEM = 56 * 1024 * 1024

f32 = jnp.float32
bf16 = jnp.bfloat16


def params():
    return pltpu.CompilerParams(vmem_limit_bytes=VMEM)


def cost(flops, moved, special=0):
    return pl.CostEstimate(flops=int(flops * 12), bytes_accessed=int(moved * 12), transcendentals=int(special * 12))


ANY = pl.BlockSpec(memory_space=pl.ANY)


def mm(a, b):
    return jnp.dot(a, b, preferred_element_type=f32)


def mm_nt(a, b):
    return lax.dot_general(a, b, (((1,), (1,)), ((), ())), preferred_element_type=f32)


def mm_tn(a, b):
    return lax.dot_general(a, b, (((0,), (0,)), ((), ())), preferred_element_type=f32)


def place(parts, starts, out_shape, puts):
    count = len(puts)

    def kernel(starts_ref, *refs):
        ins, out, held, sems_in, sems_out = refs[: len(parts)], *refs[len(parts) :]
        arriving, leaving = [], []
        for n, (part, which, where) in enumerate(puts):
            arriving.append(pltpu.make_async_copy(ins[part], where(held, starts_ref[which]), sems_in.at[n]))
            arriving[-1].start()
        for n, (part, which, where) in enumerate(puts):
            start = starts_ref[which]
            arriving[n].wait()
            leaving.append(pltpu.make_async_copy(where(held, start), where(out, start), sems_out.at[n]))
            leaving[-1].start()
        for copy in leaving:
            copy.wait()

    size = sum(p.size * p.dtype.itemsize for p in parts)
    return pl.pallas_call(
        kernel,
        grid_spec=pltpu.PrefetchScalarGridSpec(
            num_scalar_prefetch=1,
            grid=(1,),
            in_specs=[pl.BlockSpec(memory_space=pl.ANY)] * len(parts),
            out_specs=pl.BlockSpec(memory_space=pl.ANY),
            scratch_shapes=[
                pltpu.VMEM(out_shape.shape, out_shape.dtype),
                pltpu.SemaphoreType.DMA((count,)),
                pltpu.SemaphoreType.DMA((count,)),
            ],
        ),
        out_shape=out_shape,
        compiler_params=params(),
        cost_estimate=cost(0, 2 * size),
    )(starts, *parts)


def attention_forward(qkv, lengths):
    seqs, slots, three = qkv.shape
    pairs = three // (3 * PAIR)

    def kernel(len_ref, qkv_ref, out_ref, lse_ref):
        valid_count = len_ref[pl.program_id(0)]
        q2 = qkv_ref[0, :, 0:PAIR]
        k2 = qkv_ref[0, :, PAIR : 2 * PAIR]
        vt = qkv_ref[0, :, 2 * PAIR : 3 * PAIR].T
        lane = lax.broadcasted_iota(jnp.int32, (slots, PAIR), 1)
        row = lax.broadcasted_iota(jnp.int32, (slots, slots), 0)
        halves = []
        for h in range(2):
            qh = jnp.where((lane < HEAD_DIM) == (h == 0), q2, jnp.zeros_like(q2))
            st = mm_nt(k2, qh) * (SCALE * LOG2E)
            st = jnp.where(row < valid_count, st, -1e30)
            top = jnp.max(st, axis=0, keepdims=True)
            p = jnp.exp2(st - top)
            total = jnp.sum(p, axis=0, keepdims=True)
            p_low = (p * (1.0 / total)).astype(bf16)
            halves.append(mm(vt[h * HEAD_DIM : (h + 1) * HEAD_DIM, :], p_low))
            lse_ref[0, 0, h : h + 1, :] = top + jnp.log2(total)
        out_ref[0] = jnp.concatenate(halves, axis=0).T.astype(bf16)

    grid_spec = pltpu.PrefetchScalarGridSpec(
        num_scalar_prefetch=1,
        grid=(seqs, pairs),
        in_specs=[pl.BlockSpec((1, slots, 3 * PAIR), lambda s, j, n: (s, 0, j))],
        out_specs=[
            pl.BlockSpec((1, slots, PAIR), lambda s, j, n: (s, 0, j)),
            pl.BlockSpec((1, 1, 2, slots), lambda s, j, n: (s, j, 0, 0)),
        ],
    )
    work = seqs * pairs * 2 * slots * slots
    return pl.pallas_call(
        kernel,
        grid_spec=grid_spec,
        out_shape=[
            jax.ShapeDtypeStruct((seqs, slots, pairs * PAIR), bf16),
            jax.ShapeDtypeStruct((seqs, pairs, 2, slots), f32),
        ],
        compiler_params=params(),
        cost_estimate=cost(work * 4 * PAIR * 2, qkv.size * 2.7, work),
    )(lengths, qkv)


def attention_backward(qkv, grad_heads, lse, lengths, seq, waits=()):
    _, slots, three = qkv.shape
    pairs = three // (3 * PAIR)

    def kernel(len_ref, qkv_ref, gh_ref, lse_ref, *refs):
        out_ref, sums_ref = refs[-2:]
        valid_count = len_ref[seq]
        q2 = qkv_ref[0, :, 0:PAIR]
        k2 = qkv_ref[0, :, PAIR : 2 * PAIR]
        v2 = qkv_ref[0, :, 2 * PAIR : 3 * PAIR]
        g2 = gh_ref[...]
        kt = k2.T
        lane = lax.broadcasted_iota(jnp.int32, (slots, PAIR), 1)
        row = lax.broadcasted_iota(jnp.int32, (slots, slots), 0)
        grad_k, grad_v, grad_q = [], [], []
        for h in range(2):
            mine = (lane < HEAD_DIM) == (h == 0)
            qh = jnp.where(mine, q2, jnp.zeros_like(q2))
            gh = jnp.where(mine, g2, jnp.zeros_like(g2))
            st = mm_nt(k2, qh) * (SCALE * LOG2E)
            p = jnp.exp2(st - lse_ref[0, 0, h : h + 1, :])
            p = jnp.where(row < valid_count, p, 0.0)
            dp = mm_nt(v2, gh)
            inner_sum = jnp.sum(p * dp, axis=0, keepdims=True)
            ds = (p * (dp - inner_sum)).astype(bf16)
            grad_v.append(mm(p.astype(bf16), g2))
            grad_k.append(mm(ds, q2))
            grad_q.append(mm(kt[h * HEAD_DIM : (h + 1) * HEAD_DIM, :], ds))
        gq = (jnp.concatenate(grad_q, axis=0).T * SCALE).astype(bf16)
        gk = (jnp.where(lane < HEAD_DIM, grad_k[0], grad_k[1]) * SCALE).astype(bf16)
        gv = jnp.where(lane < HEAD_DIM, grad_v[0], grad_v[1]).astype(bf16)
        out_ref[:, 0:PAIR] = gq
        out_ref[:, PAIR : 2 * PAIR] = gk
        out_ref[:, 2 * PAIR : 3 * PAIR] = gv
        sums_ref[0, 0:1, :] = jnp.sum(gq.astype(f32), axis=0, keepdims=True)
        sums_ref[0, 1:2, :] = jnp.sum(gv.astype(f32), axis=0, keepdims=True)

    grid_spec = pltpu.PrefetchScalarGridSpec(
        num_scalar_prefetch=1,
        grid=(pairs,),
        in_specs=[
            pl.BlockSpec((1, slots, 3 * PAIR), lambda j, n: (seq, 0, j)),
            pl.BlockSpec((slots, PAIR), lambda j, n: (seq, j)),
            pl.BlockSpec((1, 1, 2, slots), lambda j, n: (seq, j, 0, 0)),
        ]
        + [ANY] * len(waits),
        out_specs=[
            pl.BlockSpec((slots, 3 * PAIR), lambda j, n: (0, j)),
            pl.BlockSpec((1, 2, PAIR), lambda j, n: (j, 0, 0)),
        ],
    )
    work = pairs * 2 * slots * slots
    return pl.pallas_call(
        kernel,
        grid_spec=grid_spec,
        out_shape=[
            jax.ShapeDtypeStruct((slots, three), bf16),
            jax.ShapeDtypeStruct((pairs, 2, PAIR), f32),
        ],
        compiler_params=params(),
        cost_estimate=cost(work * 10 * PAIR * 2, slots * three * 5, work),
    )(lengths, qkv, grad_heads, lse, *waits)


def project(x, w, bias, waits=(), cols=768):
    rows, depth = x.shape
    width = bias.shape[1]

    def kernel(x_ref, w_ref, b_ref, *refs):
        refs[-1][...] = (mm(x_ref[...], w_ref[...]) + b_ref[...]).astype(bf16)

    return pl.pallas_call(
        kernel,
        grid=(width // cols,),
        in_specs=[
            pl.BlockSpec((rows, depth), lambda j: (0, 0)),
            pl.BlockSpec((depth, cols), lambda j: (0, j)),
            pl.BlockSpec((1, cols), lambda j: (0, j)),
        ]
        + [ANY] * len(waits),
        out_specs=pl.BlockSpec((rows, cols), lambda j: (0, j)),
        out_shape=jax.ShapeDtypeStruct((rows, width), bf16),
        compiler_params=params(),
        cost_estimate=cost(2 * rows * depth * width, 2 * (x.size + depth * width + rows * width)),
    )(x, w, bias, *waits)


def normed(summed):
    centred = summed - jnp.mean(summed, axis=-1, keepdims=True)
    rstd = lax.rsqrt(jnp.mean(centred * centred, axis=-1, keepdims=True) + EPS)
    return centred * rstd, rstd


def norm_back(grad_hat, hat, rstd):
    return rstd * (
        grad_hat
        - jnp.mean(grad_hat, axis=-1, keepdims=True)
        - hat * jnp.mean(grad_hat * hat, axis=-1, keepdims=True)
    )


def joined(w_ref, c, cols=slice(None)):
    part = w_ref[:, c, :, cols]
    return part.reshape(part.shape[0] * part.shape[1], part.shape[2])


def reordered(ref, features, first=0, count=8, block=128):
    parts = []
    for k in range(first, first + count):
        start = pl.multiple_of(features[k] * block, block)
        parts.append(ref[:, pl.ds(start, block)].T)
    return jnp.concatenate(parts, axis=0)


def out_forward(heads, w_mid, x, b_out, gain, shift, features, rows=256):
    total, width = x.shape
    blocks, ctx, depth, _ = w_mid.shape
    cols = width // ctx

    def kernel(feat_ref, h_ref, w_ref, x_ref, b_ref, g_ref, s_ref, hat_ref, rstd_ref, low_ref, turned_ref):
        h = h_ref[...]
        attended = jnp.concatenate([mm(h, joined(w_ref, c)) for c in range(ctx)], axis=1)
        summed = attended + b_ref[...] + x_ref[...].astype(f32)
        hat, rstd = normed(summed)
        hat_ref[...] = hat
        rstd_ref[...] = rstd
        low_ref[...] = (hat * g_ref[...] + s_ref[...]).astype(bf16)
        turned_ref[...] = reordered(low_ref, feat_ref)

    block = pl.BlockSpec((rows, width), lambda i, f: (i, 0))
    vec = pl.BlockSpec((1, width), lambda i, f: (0, 0))
    weight = pl.BlockSpec((blocks, ctx, depth, cols), lambda i, f: (0, 0, 0, 4))
    grid_spec = pltpu.PrefetchScalarGridSpec(
        num_scalar_prefetch=1,
        grid=(total // rows,),
        in_specs=[block, weight, block, vec, vec, vec],
        out_specs=[
            block,
            pl.BlockSpec((rows, 1), lambda i, f: (i, 0)),
            block,
            pl.BlockSpec((width, rows), lambda i, f: (0, i)),
        ],
    )
    return pl.pallas_call(
        kernel,
        grid_spec=grid_spec,
        out_shape=[
            jax.ShapeDtypeStruct((total, width), f32),
            jax.ShapeDtypeStruct((total, 1), f32),
            jax.ShapeDtypeStruct((total, width), bf16),
            jax.ShapeDtypeStruct((width, total), bf16),
        ],
        compiler_params=params(),
        cost_estimate=cost(2 * total * width * width, total * width * 12 + width * width * 2),
    )(features, heads, w_mid, x, b_out, gain, shift)


def gelu_pair(x):
    density = jnp.exp2(x * x * (-0.5 * LOG2E))
    t = 1.0 / (jnp.abs(x) * (0.3275911 * 0.7071067811865476) + 1.0)
    poly = 1.061405429 * 0.5
    for coefficient in (-1.453152027, 1.421413741, -0.284496736, 0.254829592):
        poly = poly * t + coefficient * 0.5
    tail = poly * t * density
    phi = jnp.where(x < 0, tail, 1.0 - tail)
    active = x * phi
    slope = phi + x * density * 0.3989422804014327
    return active, slope


def ffn_one(hidden, w_mid, b_inner, cols=1024, chunk=256):
    rows, depth = hidden.shape
    width = b_inner.shape[1]
    blocks, ctx, deep, _ = w_mid.shape
    per = width // ctx // cols

    def kernel(h_ref, w_ref, b_ref, act_ref, slope_ref):
        w = joined(w_ref, 0)
        for c in range(rows // chunk):
            part = pl.ds(c * chunk, chunk)
            inner = mm(h_ref[part, :], w) + b_ref[...]
            active, slope = gelu_pair(inner)
            act_ref[part, :] = active.astype(bf16)
            slope_ref[part, :] = slope.astype(bf16)

    out = pl.BlockSpec((rows, cols), lambda j: (0, j))
    return pl.pallas_call(
        kernel,
        grid=(width // cols,),
        in_specs=[
            pl.BlockSpec((rows, depth), lambda j: (0, 0)),
            pl.BlockSpec((blocks, 1, deep, cols), lambda j: (0, j // per, 0, j % per)),
            pl.BlockSpec((1, cols), lambda j: (0, j)),
        ],
        out_specs=[out, out],
        out_shape=[jax.ShapeDtypeStruct((rows, width), bf16)] * 2,
        compiler_params=params(),
        cost_estimate=cost(2 * rows * depth * width, 2 * (hidden.size + depth * width + 2 * rows * width), 2 * rows * width),
    )(hidden, w_mid, b_inner)


def ffn_two(active, w_outer, hat_one, cot, lengths, vectors, slots, rows=256):
    total, depth = active.shape
    width = hat_one.shape[1]
    ctx = w_outer.shape[1]
    per_seq = slots // rows

    def kernel(len_ref, a_ref, w_ref, hat_ref, cot_ref, vec_ref, mixed_ref, grad_ref, low_ref, sums_ref):
        i = pl.program_id(0)
        g_one, s_one, b_outer, g_two, s_two = (vec_ref[k : k + 1, :] for k in range(5))
        a = a_ref[...]
        outer = jnp.concatenate([mm(a, joined(w_ref, c)) for c in range(ctx)], axis=1)
        summed = outer + b_outer + (hat_ref[...] * g_one + s_one)
        hat, rstd = normed(summed)
        mixed_ref[...] = (hat * g_two + s_two).astype(bf16)
        slot = (i % per_seq) * rows + lax.broadcasted_iota(jnp.int32, (rows, width), 0)
        grad_y = jnp.where(slot < len_ref[i // per_seq], cot_ref[...].astype(f32), 0.0)
        grad = norm_back(grad_y * g_two, hat, rstd)
        grad_ref[...] = grad
        low = grad.astype(bf16)
        low_ref[...] = low

        @pl.when(i == 0)
        def _():
            sums_ref[...] = jnp.zeros_like(sums_ref)

        sums_ref[0:1, :] += jnp.sum(grad_y * hat, axis=0, keepdims=True)
        sums_ref[1:2, :] += jnp.sum(grad_y, axis=0, keepdims=True)
        sums_ref[2:3, :] += jnp.sum(low.astype(f32), axis=0, keepdims=True)

    block = pl.BlockSpec((rows, width), lambda i, n: (i, 0))
    grid_spec = pltpu.PrefetchScalarGridSpec(
        num_scalar_prefetch=1,
        grid=(total // rows,),
        in_specs=[
            pl.BlockSpec((rows, depth), lambda i, n: (i, 0)),
            pl.BlockSpec(w_outer.shape, lambda i, n: (0, 0, 0, 0)),
            block,
            block,
            pl.BlockSpec((8, width), lambda i, n: (0, 0)),
        ],
        out_specs=[block, block, block, pl.BlockSpec((8, width), lambda i, n: (0, 0))],
    )
    return pl.pallas_call(
        kernel,
        grid_spec=grid_spec,
        out_shape=[
            jax.ShapeDtypeStruct((total, width), bf16),
            jax.ShapeDtypeStruct((total, width), f32),
            jax.ShapeDtypeStruct((total, width), bf16),
            jax.ShapeDtypeStruct((8, width), f32),
        ],
        compiler_params=params(),
        cost_estimate=cost(2 * total * width * depth, active.size * 2 + w_outer.size * 2 + total * width * 14),
    )(lengths, active, w_outer, hat_one, cot, vectors)


def lay(ref, value):
    blocks, ctx, parts, rows, cols = ref.shape
    for c in range(ctx):
        for k in range(parts):
            start = (c * parts + k) * cols
            ref[:, c, k] = value[:, start : start + cols].reshape(blocks, rows, cols)


def flat(array):
    blocks, ctx, parts, rows, cols = array.shape
    return array.transpose(0, 3, 1, 2, 4).reshape(blocks * rows, ctx * parts * cols)


def ffn_back(grad_low, start, hidden_t, active, slope, w_outer, w_mid, order, waits=(), cols=512):
    rows, width = grad_low.shape
    count = order.shape[0]
    half = width // 2
    blocks, ctx, deep, _ = w_mid.shape
    per = active.shape[1] // ctx // cols
    outer_rows = w_outer.shape[2]
    outer_cols = w_outer.shape[3]

    def kernel(ord_ref, g_ref, start_ref, ht_ref, a_ref, s_ref, wo_ref, wi_ref, *refs):
        grad_ref, dwo_ref, dws_ref, dwk_ref, bias_ref = refs[-5:]
        j = pl.program_id(0)
        grad = g_ref[...]
        grad_active = sum(
            mm_nt(grad[:, c * outer_cols : (c + 1) * outer_cols], joined(wo_ref, c)) for c in range(ctx)
        )
        inner = (grad_active * s_ref[...].astype(f32)).astype(bf16)
        bias_ref[...] = jnp.sum(inner.astype(f32), axis=0, keepdims=True)
        lay(dwo_ref, mm_tn(a_ref[...], grad).astype(bf16))
        lay(dws_ref, mm(ht_ref[0:half, :], inner).astype(bf16))
        lay(dwk_ref, mm(ht_ref[half:width, :], inner).astype(bf16))

        @pl.when(j == 0)
        def _():
            grad_ref[...] = start_ref[...]

        grad_ref[...] += mm_nt(inner, joined(wi_ref, 0))

    whole = lambda j, o: (0, 0)
    grid_spec = pltpu.PrefetchScalarGridSpec(
        num_scalar_prefetch=1,
        grid=(count,),
        in_specs=[
            pl.BlockSpec((rows, width), whole),
            pl.BlockSpec((rows, width), whole),
            pl.BlockSpec((width, rows), whole),
            pl.BlockSpec((rows, cols), lambda j, o: (0, o[j])),
            pl.BlockSpec((rows, cols), lambda j, o: (0, o[j])),
            pl.BlockSpec((cols // outer_rows, ctx, outer_rows, outer_cols), lambda j, o: (o[j], 0, 0, 0)),
            pl.BlockSpec((blocks, 1, deep, cols), lambda j, o: (0, o[j] // per, 0, o[j] % per)),
        ]
        + [ANY] * len(waits),
        out_specs=[
            pl.BlockSpec((rows, width), whole),
            pl.BlockSpec((1, ctx, 1, cols, outer_cols), lambda j, o: (j, 0, 0, 0, 0)),
            pl.BlockSpec((4, 1, cols // 256, half // 4, 256), lambda j, o: (0, j, 0, 0, 0)),
            pl.BlockSpec((4, 1, cols // 256, half // 4, 256), lambda j, o: (0, j, 0, 0, 0)),
            pl.BlockSpec((1, cols), lambda j, o: (0, j)),
        ],
    )
    return pl.pallas_call(
        kernel,
        grid_spec=grid_spec,
        out_shape=[
            jax.ShapeDtypeStruct((rows, width), f32),
            jax.ShapeDtypeStruct((count, ctx, 1, cols, outer_cols), bf16),
            jax.ShapeDtypeStruct((4, count, cols // 256, half // 4, 256), bf16),
            jax.ShapeDtypeStruct((4, count, cols // 256, half // 4, 256), bf16),
            jax.ShapeDtypeStruct((1, count * cols), f32),
        ],
        compiler_params=params(),
        cost_estimate=cost(8 * rows * width * count * cols, 12 * count * cols * width + 12 * rows * width),
    )(order, grad_low, start, hidden_t, active, slope, w_outer, w_mid, *waits)


def out_back(grad_hidden, hat, rstd, gain, w_mid, heads, features, waits=(), rows=256):
    total, width = grad_hidden.shape
    half = width // 2
    steps = total // rows
    blocks, ctx, depth, _ = w_mid.shape
    cols = width // ctx

    def kernel(feat_ref, gh_ref, hat_ref, rstd_ref, gain_ref, w_ref, h_ref, *refs):
        one_ref, heads_ref, dws_ref, dwk_ref, sums_ref, acc = refs[-6:]
        i = pl.program_id(0)
        grad_y = gh_ref[...]
        hat = hat_ref[...]
        grad = norm_back(grad_y * gain_ref[...], hat, rstd_ref[...])
        one_ref[...] = grad
        low = grad.astype(bf16)
        heads_ref[...] = sum(mm_nt(low[:, c * cols : (c + 1) * cols], joined(w_ref, c)) for c in range(ctx)).astype(bf16)

        @pl.when(i == 0)
        def _():
            sums_ref[...] = jnp.zeros_like(sums_ref)
            acc[...] = jnp.zeros_like(acc)

        acc[...] += mm(reordered(h_ref, feat_ref), low)
        sums_ref[0:1, :] += jnp.sum(grad_y * hat, axis=0, keepdims=True)
        sums_ref[1:2, :] += jnp.sum(grad_y, axis=0, keepdims=True)
        sums_ref[2:3, :] += jnp.sum(low.astype(f32), axis=0, keepdims=True)

        @pl.when(i == steps - 1)
        def _():
            lay(dws_ref, acc[0:half, :].astype(bf16))
            lay(dwk_ref, acc[half:width, :].astype(bf16))

    block = pl.BlockSpec((rows, width), lambda i, f: (i, 0))
    whole = lambda i, f: (0, 0)
    grid_spec = pltpu.PrefetchScalarGridSpec(
        num_scalar_prefetch=1,
        grid=(steps,),
        in_specs=[
            block,
            block,
            pl.BlockSpec((rows, 1), lambda i, f: (i, 0)),
            pl.BlockSpec((1, width), whole),
            pl.BlockSpec((blocks, ctx, depth, cols), lambda i, f: (0, 0, 0, 4)),
            block,
        ]
        + [ANY] * len(waits),
        out_specs=[
            block,
            block,
            pl.BlockSpec((4, ctx, 1, half // 4, cols), lambda i, f: (0, 0, 0, 0, 0)),
            pl.BlockSpec((4, ctx, 1, half // 4, cols), lambda i, f: (0, 0, 0, 0, 0)),
            pl.BlockSpec((8, width), whole),
        ],
        scratch_shapes=[pltpu.VMEM((width, width), f32)],
    )
    return pl.pallas_call(
        kernel,
        grid_spec=grid_spec,
        out_shape=[
            jax.ShapeDtypeStruct((total, width), f32),
            jax.ShapeDtypeStruct((total, width), bf16),
            jax.ShapeDtypeStruct((4, ctx, 1, half // 4, cols), bf16),
            jax.ShapeDtypeStruct((4, ctx, 1, half // 4, cols), bf16),
            jax.ShapeDtypeStruct((8, width), f32),
        ],
        compiler_params=params(),
        cost_estimate=cost(4 * total * width * width, total * width * 16 + width * width * 4),
    )(features, grad_hidden, hat, rstd, gain, w_mid, heads, *waits)


def attn_weight_grads(x, grads, features, part, got=None, waits=(), cols=768):
    total, width = x.shape
    count = len(grads)
    slots, three = grads[0].shape
    half = width // 2
    blocks = half // 128

    def kernel(feat_ref, x_ref, *refs):
        out_ref, turned = refs[-2:]

        @pl.when(pl.program_id(0) == 0)
        def _():
            turned[...] = reordered(x_ref, feat_ref, part * blocks, blocks)

        value = sum(mm(turned[:, n * slots : (n + 1) * slots], refs[n][...]) for n in range(count))
        if got is not None:
            value = value + refs[count][...].reshape(half, cols).astype(f32)
        lay(out_ref, value.astype(bf16))

    column = pl.BlockSpec((slots, cols), lambda j, f: (0, j))
    out = pl.BlockSpec((4, 1, 1, half // 4, cols), lambda j, f: (0, j, 0, 0, 0))
    extra = [] if got is None else [got]
    grid_spec = pltpu.PrefetchScalarGridSpec(
        num_scalar_prefetch=1,
        grid=(three // cols,),
        in_specs=[pl.BlockSpec((total, width), lambda j, f: (0, 0))]
        + [column] * count
        + [out] * len(extra)
        + [ANY] * len(waits),
        out_specs=out,
        scratch_shapes=[pltpu.VMEM((half, total), bf16)],
    )
    return pl.pallas_call(
        kernel,
        grid_spec=grid_spec,
        out_shape=jax.ShapeDtypeStruct((4, three // cols, 1, half // 4, cols), bf16),
        compiler_params=params(),
        cost_estimate=cost(total * width * three, 2 * (total * width + total * three + width * three)),
    )(features, x, *grads, *extra, *waits)


def token_grads(grad_qkv, w_attn, grad_one, seq, waits=(), rows=256):
    slots, three = grad_qkv.shape
    width = grad_one.shape[1]
    steps = slots // rows

    def kernel(g_ref, w_ref, one_ref, *refs):
        refs[-1][...] = (mm_nt(g_ref[...], w_ref[...]) + one_ref[...]).astype(bf16)

    return pl.pallas_call(
        kernel,
        grid=(steps,),
        in_specs=[
            pl.BlockSpec((rows, three), lambda i: (i, 0)),
            pl.BlockSpec((width, three), lambda i: (0, 0)),
            pl.BlockSpec((rows, width), lambda i: (seq * steps + i, 0)),
        ]
        + [ANY] * len(waits),
        out_specs=pl.BlockSpec((rows, width), lambda i: (i, 0)),
        out_shape=jax.ShapeDtypeStruct((slots, width), bf16),
        compiler_params=params(),
        cost_estimate=cost(2 * slots * three * width, 2 * (slots * three + width * three) + slots * width * 6),
    )(grad_qkv, w_attn, grad_one, *waits)


def swap(array, axis, size, mask):
    return lax.ppermute(array, axis, [(i, i ^ mask) for i in range(size)])


def shift(array, axis, size, by):
    return lax.ppermute(array, axis, [(i, (i + by) % size) for i in range(size)])


def after(array, *earlier):
    return lax.optimization_barrier((array, *earlier))[0]


def after_all(array, earlier):
    return after(array, *earlier) if earlier else array


class Columns:
    def __init__(self, shard, c):
        self.c, self.shard = c, shard

    def first(self):
        self.near = swap(self.shard, "ctx", 4, 1)
        return self.near

    def second(self):
        odd = (self.c & 1) == 1
        self.pair = jnp.stack(
            [jnp.where(odd, self.near, self.shard), jnp.where(odd, self.shard, self.near)]
        )
        self.across = lax.ppermute(self.pair, "ctx", [(1, 2), (2, 1)])
        return self.across

    def third(self):
        self.outwards = lax.ppermute(self.across, "ctx", [(1, 0), (2, 3)])
        return self.outwards

    def pieces(self):
        middle = (self.c == 1) | (self.c == 2)
        other = jnp.where(middle, self.across, self.outwards)
        upper = self.c >= 2
        return jnp.concatenate([jnp.where(upper, other, self.pair), jnp.where(upper, self.pair, other)])


def gather_rows(block, r, dp):
    if dp != 8:
        return lax.all_gather(block, "dp", axis=0, tiled=True), ()
    rows, width = block.shape
    half = rows // 2
    by_x = swap(block, "dp", dp, 2)
    by_y = swap(block, "dp", dp, 4)
    far_top = swap(by_x[:half], "dp", dp, 4)
    far_low = swap(by_y[half:], "dp", dp, 2)
    own = [block, by_x, by_y, far_top, far_low]
    twin = [swap(part, "dp", dp, 1) for part in own]

    def at(offset, count):
        return lambda out, start: out.at[pl.ds(pl.multiple_of(start + offset, half), count), :]

    puts = []
    for n, base in ((0, 0), (5, 1)):
        puts += [
            (n, base, at(0, rows)),
            (n + 1, base ^ 2, at(0, rows)),
            (n + 2, base ^ 4, at(0, rows)),
            (n + 3, base ^ 6, at(0, half)),
            (n + 4, base ^ 6, at(half, half)),
        ]
    starts = jnp.stack([(r ^ m) * rows for m in range(8)]).astype(jnp.int32)
    shape = jax.ShapeDtypeStruct((dp * rows, width), block.dtype)
    return place(own + twin, starts, shape, puts), (by_x, by_y)


class Exchange:
    def __init__(self, array, c, ctx, gather):
        self.c, self.ctx, self.gather = c, ctx, gather
        if gather:
            seqs, self.count, self.width = array.shape
            self.per = seqs // ctx
        else:
            self.per, total, self.width = array.shape
            self.count = total // ctx
        self.dtype = array.dtype
        self.parts = [self.piece(array, (c + d) % ctx) for d in range(ctx)]
        self.pieces = tuple(self.parts)

    def piece(self, array, index):
        start = (index * self.per, 0, 0) if self.gather else (0, index * self.count, 0)
        return lax.dynamic_slice(array, start, (self.per, self.count, self.width))

    def send(self, *which):
        for d in which or range(1, self.ctx):
            self.parts[d] = shift(self.parts[d], "ctx", self.ctx, d)
        return self.parts

    def arrive(self, *earlier):
        self.parts = list(lax.optimization_barrier((*self.parts, *earlier))[: self.ctx])

    def placed(self):
        step = self.count if self.gather else self.per
        starts = jnp.stack([((self.c - d) % self.ctx) * step for d in range(self.ctx)]).astype(jnp.int32)
        if self.gather:
            at = lambda out, start: out.at[:, pl.ds(pl.multiple_of(start, step), step), :]
            shape = (self.per, self.ctx * self.count, self.width)
        else:
            at = lambda out, start: out.at[pl.ds(start, step), :, :]
            shape = (self.per * self.ctx, self.count, self.width)
        return place(self.parts, starts, jax.ShapeDtypeStruct(shape, self.dtype), [(d, d, at) for d in range(self.ctx)])


class RowSum:
    def __init__(self, parts, r, dp):
        self.parts, self.dp = parts, dp
        self.y, self.x = (r >> 2) & 1, (r >> 1) & 1

    def pick(self, array, yi, xi, h):
        _, ctx, parts, rows, width = array.shape
        array = array.reshape(2, 2, 2, ctx // 2, parts, rows, width)
        start = (0 if yi is None else yi, 0 if xi is None else xi, h, 0, 0, 0, 0)
        sizes = (2 if yi is None else 1, 2 if xi is None else 1, 1, ctx // 2, parts, rows, width)
        out = lax.dynamic_slice(array, tuple(jnp.int32(s) for s in start), sizes)
        return out.reshape(sizes[0] * sizes[1], *sizes[3:]).astype(f32)

    def summed(self, yi, xi, h):
        sums = [
            self.pick(kept, yi, xi, h) if got is None else self.pick(got, yi, xi, h) + self.pick(kept, yi, xi, h)
            for got, kept in self.parts
        ]
        return sums[0] if len(sums) == 1 else jnp.concatenate(sums, axis=2)

    def pack(self, array):
        return array.astype(bf16)

    def plus(self, array, packed, index=None):
        if index is not None:
            packed = lax.dynamic_slice_in_dim(packed, index, 1, axis=0)
        return array + packed.astype(f32)

    def first_sends(self):
        self.sends = (self.pack(self.summed(None, 1 - self.x, 0)), self.pack(self.summed(1 - self.y, None, 1)))
        return self.sends

    def first(self):
        self.got_x = swap(self.sends[0], "dp", self.dp, 2)
        self.got_y = swap(self.sends[1], "dp", self.dp, 4)
        return (self.got_x, self.got_y)

    def first_there(self, *earlier):
        self.got_x, self.got_y = lax.optimization_barrier((self.got_x, self.got_y, *earlier))[:2]

    def second_there(self, *earlier):
        self.top, self.low = lax.optimization_barrier((self.top, self.low, *earlier))[:2]

    def second_sends(self):
        y, x = self.y, self.x
        self.sends = (
            self.pack(self.plus(self.summed(1 - y, x, 0), self.got_x, 1 - y)),
            self.pack(self.plus(self.summed(y, 1 - x, 1), self.got_y, 1 - x)),
        )
        return self.sends

    def second(self):
        self.top = swap(self.sends[0], "dp", self.dp, 4)
        self.low = swap(self.sends[1], "dp", self.dp, 2)
        return (self.top, self.low)

    def result(self):
        y, x = self.y, self.x
        top = self.plus(self.plus(self.summed(y, x, 0), self.got_x, y), self.top)
        low = self.plus(self.plus(self.summed(y, x, 1), self.got_y, x), self.low)
        return jnp.concatenate([top[0], low[0]], axis=0)


class ColumnSum:
    def __init__(self, blocks, c):
        self.blocks = blocks
        self.pair, self.odd = c >> 1, c & 1

    def columns(self, array, index, count):
        return lax.dynamic_slice_in_dim(array, index * count, count, axis=0)

    def first_send(self):
        self.other = self.columns(self.blocks, 1 - self.pair, 2)
        self.send = self.other.astype(bf16)
        return self.send

    def first(self):
        self.got = lax.ppermute(self.send, "ctx", [(0, 1), (3, 2)])
        return self.got

    def there(self, *earlier):
        self.got = after(self.got, *earlier)

    def second_send(self):
        self.send = (self.other + self.got.astype(f32)).astype(bf16)
        return self.send

    def second(self):
        self.got = lax.ppermute(self.send, "ctx", [(1, 2), (2, 1)])
        return self.got

    def third_send(self):
        self.mine = self.columns(self.blocks, self.pair, 2) + self.got.astype(f32)
        self.send = self.columns(self.mine, 1 - self.odd, 1).astype(bf16)
        return self.send

    def third(self):
        self.got = swap(self.send, "ctx", 4, 1)
        return self.got

    def result(self):
        return (self.columns(self.mine, self.odd, 1) + self.got.astype(f32))[0]

    def whole(self):
        for stage in ("first", "second", "third"):
            getattr(self, stage + "_send")()
            getattr(self, stage)()
        return self.result()


def side_by_side(parts):
    return jnp.concatenate([parts[k] for k in range(parts.shape[0])], axis=1)


def pair_columns(query, key, value):
    rows, width = query.shape
    pieces = []
    for j in range(width // PAIR):
        pieces += [a[:, j * PAIR : (j + 1) * PAIR] for a in (query, key, value)]
    return jnp.concatenate(pieces, axis=1)


def on_device(
    dp,
    ctx,
    tokens,
    lengths,
    cotangent,
    weight_query,
    weight_key,
    weight_value,
    weight_out,
    weight_inner,
    weight_outer,
    bias_query,
    bias_value,
    bias_out,
    bias_inner,
    bias_outer,
    gain_attn,
    shift_attn,
    gain_ffn,
    shift_ffn,
):
    seq_total, slot_count, width = tokens.shape
    units = bias_inner.shape[0]
    per = seq_total // ctx
    slots = slot_count * ctx
    rows = per * slots
    c = lax.axis_index("ctx")
    r = lax.axis_index("dp")
    core = r & 1
    paired = dp == 8

    own_lengths = lax.dynamic_slice(lengths, (c * per,), (per,))
    attn_shard = pair_columns(weight_query, weight_key, weight_value)
    attn = Columns(attn_shard, c)
    mid = Columns(jnp.concatenate([weight_inner, weight_out], axis=1), c)
    outer = Columns(weight_outer, c)
    attn.first()
    mid.shard = after(mid.shard, attn.near)
    attn.second()
    mid.first()
    attn.across, mid.near, outer.shard = lax.optimization_barrier((attn.across, mid.near, outer.shard))
    attn.third()
    mid.second()
    outer.first()
    attn.outwards, mid.across, outer.near, tokens = lax.optimization_barrier(
        (attn.outwards, mid.across, outer.near, tokens)
    )
    mid.third()
    outer.second()
    x = Exchange(tokens, c, ctx, True)
    x.send(2)
    block = jnp.concatenate([p for p in attn.pieces()], axis=1)
    w_attn, early = gather_rows(block, r, dp)
    x.parts[1], x.parts[3], mid.outwards, outer.across = lax.optimization_barrier(
        (x.parts[1], x.parts[3], mid.outwards, outer.across)
    )
    x.send(1, 3)
    w_mid = lax.all_gather(after_all(mid.pieces(), early), "dp", axis=0)
    outer.across = after(outer.across, x.parts[2])
    outer.third()
    x.arrive(outer.outwards)
    x = x.placed().reshape(rows, width)
    cot = Exchange(after(cotangent, x), c, ctx, True)
    cot.send()

    if paired:
        order_s = (jnp.arange(4) * 2 + (1 - core)).astype(jnp.int32)
        order_k = (jnp.arange(4) * 2 + core).astype(jnp.int32)
    else:
        order_s, order_k = jnp.arange(4, dtype=jnp.int32), jnp.arange(4, 8, dtype=jnp.int32)
    features = jnp.concatenate([order_s, order_k])

    bias_qkv = pair_columns(bias_query[None], jnp.zeros_like(bias_query)[None], bias_value[None])
    qkv = project(x, w_attn, bias_qkv, cot.pieces).reshape(per, slots, 3 * width)
    outer.outwards = after(outer.outwards, qkv)
    w_outer = lax.all_gather(outer.pieces(), "dp", axis=0)
    heads, lse = attention_forward(qkv, own_lengths)
    heads = heads.reshape(rows, width)
    hat_one, rstd_one, hidden_low, hidden_t = out_forward(
        heads, w_mid, x, bias_out[None], gain_attn[None], shift_attn[None], features
    )
    active, slope = ffn_one(hidden_low, w_mid, bias_inner[None])
    cot.arrive(hidden_low)
    cot = cot.placed().reshape(rows, width)
    vectors = jnp.stack([gain_attn, shift_attn, bias_outer, gain_ffn, shift_ffn] + [shift_ffn] * 3)
    mixed, grad_two, grad_outer, sums_two = ffn_two(
        active, w_outer, hat_one, cot, own_lengths, vectors, slots
    )
    mixed = Exchange(mixed.reshape(per, slots, width), c, ctx, False)
    mixed.send()

    def from_twin(sent):
        return swap(sent, "dp", dp, 1) if paired else sent

    def part(got, kept):
        return (got, kept)

    grad_hidden, outer_s, inner_s1, inner_k1, bias_1 = ffn_back(
        grad_outer, grad_two, hidden_t, active, slope, w_outer, w_mid, order_s, mixed.pieces
    )
    got_outer = from_twin(outer_s)
    grad_hidden, outer_k, inner_s2, inner_k2, bias_2 = ffn_back(
        grad_outer, grad_hidden, hidden_t, active, slope, w_outer, w_mid, order_k, (mixed.parts[3],)
    )
    got_inner_1, got_inner_2 = from_twin(inner_s2), from_twin(inner_s1)
    hold = (mixed.parts[1],)
    if paired:
        sum_c = RowSum([part(after(got_outer, outer_k), outer_k)], r, dp)
        hold = (*hold, *sum_c.first_sends())
        sum_c.first()
    grad_one, grad_heads, out_s, out_k, sums_one = out_back(
        grad_hidden, hat_one, rstd_one, gain_attn[None], w_mid, heads, features, waits=hold
    )
    got_out = from_twin(out_s)
    got_inner_1, got_inner_2, out_k = lax.optimization_barrier((got_inner_1, got_inner_2, out_k))
    mixed.arrive(out_k)
    mixed = mixed.placed()
    grad_qkv, sums_qkv, slot_grads = [], [], []
    last = per - 1
    hold = (mixed, got_inner_1, got_inner_2)
    for n in range(per):
        grad, sums = attention_backward(qkv, grad_heads, lse, own_lengths, n, waits=hold)
        grad_qkv.append(grad)
        sums_qkv.append(sums)
        hold = ()
        if paired and n == 0:
            got_out = after(got_out, grad)
            sum_b = RowSum([part(got_inner_1, inner_k1), part(got_inner_2, inner_k2), part(got_out, out_k)], r, dp)
            sum_c.first_there(grad)
            hold = (*sum_c.second_sends(), *sum_b.first_sends())
            sum_c.second()
            sum_b.first()
        if n < last:
            tokens_n = token_grads(grad, w_attn, grad_one, n, waits=hold)
            slot_grads.append(Exchange(tokens_n[None], c, ctx, False))
            hold = slot_grads[-1].pieces
            if paired and n == 0:
                sum_c.second_there(tokens_n)
                hold = (*hold, sum_c.top, sum_c.low)
            slot_grads[-1].send()
    hold = []
    for exchange in slot_grads:
        exchange.arrive(grad_qkv[last])
        hold.append(exchange.placed())
    slot_grads = list(hold)
    if paired:
        cols_c = ColumnSum(sum_c.result(), c)
        sum_b.first_there(grad_qkv[last])
        hold = [*hold, after(cols_c.first_send(), grad_qkv[last]), *sum_b.second_sends()]
        cols_c.first()
        sum_b.second()
    qkv_s = attn_weight_grads(x, grad_qkv, features, 0, waits=hold)
    got_qkv = from_twin(qkv_s)
    hold = []
    if paired:
        cols_c.there(qkv_s)
        hold.append(cols_c.second_send())
        cols_c.second()
    tokens_n = token_grads(grad_qkv[last], w_attn, grad_one, last, waits=hold)
    slots_n = Exchange(tokens_n[None], c, ctx, False)
    slots_n.send()
    if paired:
        cols_c.there(tokens_n)
        qkv_k = attn_weight_grads(x, grad_qkv, features, 1, after(got_qkv, tokens_n), slots_n.pieces)
        qkv_k, slots_n.parts[3], sum_b.top, sum_b.low = lax.optimization_barrier(
            (qkv_k, slots_n.parts[3], sum_b.top, sum_b.low)
        )
        sum_a = RowSum([(None, qkv_k)], r, dp)
        sends = sum_a.first_sends()
        sum_a.first()
        sum_b.second_there(*sends, slots_n.parts[1], slots_n.parts[2])
        cols_b = ColumnSum(sum_b.result(), c)
        cols_b.first_send()
        cols_b.first()
        sum_a.first_there(cols_b.send)
        sends = sum_a.second_sends()
        sum_a.second()
        cols_b.there(*sends)
        cols_b.second_send()
        cols_b.second()
        sum_a.second_there(cols_b.send)
        cols_a = ColumnSum(sum_a.result(), c)
        cols_a.first_send()
        cols_a.first()
        slots_n.arrive(cols_b.send)
    else:
        qkv_k = attn_weight_grads(x, grad_qkv, features, 1)
    slot_grads.append(slots_n.placed())
    grad_tokens = jnp.stack(slot_grads, axis=1)
    grad_tokens = grad_tokens.reshape(seq_total, slot_count, width).astype(f32)

    if paired:
        cols_a.second_send()
        cols_a.second()
        cols_a.third_send()
        cols_a.third()
        cols_b.there(cols_a.send)
        cols_b.third_send()
        cols_b.third()
        cols_c.there(cols_a.send)
        cols_c.third_send()
        cols_c.third()
        cols_b.there(cols_a.send)
        sum_outer = side_by_side(cols_c.result())
        rest = cols_b.result()
        inner_1, inner_2, sum_out = side_by_side(rest[0:2]), side_by_side(rest[2:4]), rest[4]
        sum_qkv = side_by_side(cols_a.result())
        sum_inner = jnp.where(
            core == 0,
            jnp.concatenate([inner_2, inner_1], axis=1),
            jnp.concatenate([inner_1, inner_2], axis=1),
        )
        b_1, b_2 = bias_1.reshape(4, -1), bias_2.reshape(4, -1)
        bias_units = jnp.where(core == 0, jnp.stack([b_2, b_1], axis=1), jnp.stack([b_1, b_2], axis=1)).reshape(units)
    else:

        def summed(*arrays):
            array = jnp.concatenate(arrays, axis=0).astype(f32)
            array = lax.psum_scatter(array, "dp", scatter_dimension=0, tiled=True)
            array = array.reshape(array.shape[0], ctx, -1).transpose(1, 0, 2)
            return ColumnSum(array, c).whole()

        sum_outer = summed(flat(outer_s), flat(outer_k))
        sum_inner = summed(
            jnp.concatenate([flat(inner_s1), flat(inner_s2)], axis=1),
            jnp.concatenate([flat(inner_k1), flat(inner_k2)], axis=1),
        )
        sum_out = summed(flat(out_s), flat(out_k))
        sum_qkv = summed(flat(qkv_s), flat(qkv_k))
        bias_units = jnp.concatenate([bias_1[0], bias_2[0]])

    own_rows = sum_qkv.shape[0]
    sum_qkv = sum_qkv.reshape(own_rows, -1, 3, PAIR)
    sum_query, sum_key, sum_value = (sum_qkv[:, :, k].reshape(own_rows, -1) for k in range(3))

    sums_qkv = sum(sums_qkv)
    packed = jnp.concatenate(
        [
            sums_qkv[:, 0].reshape(-1),
            sums_qkv[:, 1].reshape(-1),
            sums_one[2],
            bias_units,
            sums_two[2],
            sums_one[0],
            sums_one[1],
            sums_two[0],
            sums_two[1],
        ]
    )
    packed = lax.all_gather(packed.reshape(-1, 128), ("dp", "ctx"))
    if paired:
        packed = after(packed, cols_a.send)
    packed = jnp.sum(packed, axis=0).reshape(-1)
    totals, at = [], 0
    for size in (width, width, width, units, width, width, width, width, width):
        totals.append(packed[at : at + size])
        at += size
    return (mixed, grad_tokens, sum_query, sum_key, sum_value, sum_out, sum_inner, sum_outer, *totals)


def solution(mesh):
    rows = P("dp", "ctx", None)
    matrix = P("dp", "ctx")
    in_specs = (rows, P("dp"), rows) + (matrix,) * 6 + (P(),) * 9
    out_specs = (rows, rows) + (matrix,) * 6 + (P(),) * 9
    step = functools.partial(on_device, mesh.shape["dp"], mesh.shape["ctx"])
    return jax.shard_map(step, mesh=mesh, in_specs=in_specs, out_specs=out_specs, check_vma=False)
```
